32 devices in a mesh: day: 4 (over x, core), year: 4 (over z), region: 2 (over y).
Axes of the slice: x: 2, y: 2, z: 4, core: 2. Of those that a mesh axis runs over, the one named last changes fastest.
Arguments:
- samples: bfloat16 [92, 8, 2000, 256], P('day', 'year', 'region'), parts along dimension 2, may hold values from -24 to 24, as said below
- counts: int32 [2, 92, 8], P('region', 'day', 'year'), parts along dimension 0, may hold values from 500 to 1000, as said below
Outputs:
- covariance: float32 [2, 92, 256, 256], P('region', 'day', 'year'), parts along dimension 0
- window_mean: float32 [2, 92, 256], P('region', 'day', 'year'), parts along dimension 0
The draws below stay inside these ranges and needn't reach their ends.
There are 2 independent parts, one for each index of `region`. The reference program is written for one: setup_inputs(seed, part) draws one part's arguments, and reference() takes and returns one part's arrays. A program takes and returns all parts, laid end to end along the dimension named above; each array names one. Nothing has to cross between parts.
Inputs may be any that keep to these rules, and one draw needn't show every extreme that they name: `counts`: every entry lies between 500 and 1000; both ends are taken in every draw. `samples`: finite profile values.
All inputs are finite; a program needn't handle non-finite values.
Results may differ from the reference program's by a relative error of at most 0.0003.
Values sent between devices are 32-bit elements; how exact they have to be, the bound alone decides.
No kernel may reach another device: no remote copies, remote signals or barrier semaphores. Data moves between devices by JAX's collectives and lax.ppermute only.
A program may use at most 128 MiB of HBM per device.

```python
import math
import jax
import jax.numpy as jnp
from jax import lax

F = 256
HALF = 7
S = 1000
DAYS = 92
GROUPS = 8


def draw_samples(key, part):
    keys = jax.random.split(key, 3)
    shape = (DAYS, GROUPS, S, F)
    feature_scale = 0.3 * jnp.exp(jax.random.uniform(keys[1], (F,), jnp.float32, 0.0, math.log(10.0)))
    day_scale = jnp.exp(jax.random.uniform(keys[2], (DAYS, 1, 1, 1), jnp.float32, -math.log(2.0), math.log(2.0)))
    base = jax.random.truncated_normal(keys[0], -4.0, 4.0, shape, jnp.float32)
    values = base * feature_scale * day_scale
    return values.astype(jnp.bfloat16)


def draw_counts(key, part):
    values = jax.random.randint(key, (1, DAYS, GROUPS), S // 2, S + 1, dtype=jnp.int32)
    values = values.at[0, 0, 0].set(S)
    values = values.at[0, 1, 0].set(S // 2)
    return values


def setup_inputs(seed: int = 0, part: int = 0) -> dict:
    streams_of = jax.random.split(jax.random.key(seed), 3)
    own_keys = jax.random.split(jax.random.fold_in(streams_of[2], part), 3)
    return {
        "samples": draw_samples(jax.random.fold_in(jax.random.fold_in(streams_of[2], part), 71), part),
        "counts": draw_counts(jax.random.fold_in(jax.random.fold_in(streams_of[2], part), 71), part),
    }


def one_day(args):
    day_samples, day_counts = args
    slots = lax.broadcasted_iota(jnp.int32, (day_samples.shape[0], day_samples.shape[1]), 1)
    valid = slots < day_counts[:, None]
    masked = jnp.where(valid[:, :, None], day_samples, jnp.zeros_like(day_samples))
    flat = masked.reshape(-1, masked.shape[-1])
    gram = jnp.dot(flat.T, flat, preferred_element_type=jnp.float32)
    total = jnp.sum(flat, axis=0, dtype=jnp.float32)
    return gram, total


def reference(samples, counts):
    day_gram, day_sum = lax.map(one_day, (samples, counts[0]))
    day_count = jnp.sum(counts[0], axis=1).astype(jnp.float32)
    win_gram = jnp.zeros_like(day_gram)
    win_sum = jnp.zeros_like(day_sum)
    win_count = jnp.zeros_like(day_count)
    for offset in range(-HALF, HALF + 1):
        win_gram = win_gram + jnp.roll(day_gram, -offset, axis=0)
        win_sum = win_sum + jnp.roll(day_sum, -offset, axis=0)
        win_count = win_count + jnp.roll(day_count, -offset, axis=0)
    window_mean = win_sum / win_count[:, None]
    outer = win_count[:, None, None] * window_mean[:, :, None] * window_mean[:, None, :]
    covariance = (win_gram - outer) / (win_count - 1.0)[:, None, None]
    return covariance[None], window_mean[None]
```

```python
import functools

import jax
import jax.numpy as jnp
from jax import lax
from jax.experimental import pallas as pl
from jax.experimental.pallas import tpu as pltpu
from jax.sharding import PartitionSpec as P

HALF = 7
LANES = 128
BLOCK = 64
SUBLANES = 8
FULL, CROSS, OWN = 4 * BLOCK, 3 * BLOCK, 2 * BLOCK
SMALL = 3
TOKEN = (SUBLANES, LANES)
SCALARS = pl.BlockSpec(memory_space=pltpu.SMEM)
INSIDE = pl.BlockSpec(memory_space=pltpu.VMEM)
ANYWHERE = pl.BlockSpec(memory_space=pl.ANY)


def small_rows(days):
    return -(-(SMALL * days + 1) // SUBLANES) * SUBLANES


def length(runs):
    return sum(size for _, size in runs)


def call(kernel, args, specs, shapes, scratch, flops, moved, mebibytes=16, outs=None):
    results = pl.pallas_call(
        kernel,
        in_specs=list(specs),
        out_specs=(list(outs) if outs else [INSIDE] * len(shapes)) + [INSIDE],
        out_shape=[jax.ShapeDtypeStruct(shape, jnp.float32) for shape in list(shapes) + [TOKEN]],
        scratch_shapes=scratch,
        cost_estimate=pl.CostEstimate(flops=flops, bytes_accessed=moved, transcendentals=0),
        compiler_params=pltpu.CompilerParams(vmem_limit_bytes=mebibytes * 1024 * 1024),
    )(*args)
    return results[:-1], results[-1]


def iotas(shape):
    return lax.broadcasted_iota(jnp.int32, shape, 0), lax.broadcasted_iota(jnp.int32, shape, 1)


def swap(block):
    return pltpu.roll(block, BLOCK, 1)


def pack_quadrant(quadrant):
    top, bottom = quadrant[:BLOCK], swap(quadrant[BLOCK:])
    row, lane = iotas((BLOCK, LANES))
    packed = jnp.where((lane < BLOCK) & (row > lane), bottom, top)
    diagonal = jnp.sum(jnp.where(row == lane, bottom, 0.0), axis=0, keepdims=True)
    return packed, diagonal


def gram_kernel(parts, counts_ref, samples_ref, after_ref, *refs):
    outs, token_ref, held, arrived = refs[: len(parts)], *refs[len(parts) :]
    groups, slots, width = held.shape[1:]
    lane = lax.broadcasted_iota(jnp.int32, (1, LANES), 1)
    rank = lax.broadcasted_iota(jnp.int32, (2 * SUBLANES, slots), 1)
    token_ref[...] = jnp.zeros_like(token_ref)

    def copies(day, slot):
        return [
            pltpu.make_async_copy(samples_ref.at[day, g], held.at[slot, g], arrived.at[slot, g])
            for g in range(groups)
        ]

    slot = 0
    for runs in parts:
        for start, number in runs:
            for i in range(number):
                for copy in copies(start + i, slot + i):
                    copy.start()
            slot += number
    slot = 0
    for runs, out_ref in zip(parts, outs):
        days = length(runs)
        small = days * FULL
        out_ref[small:] = jnp.zeros((small_rows(days), LANES), jnp.float32)
        numbers = jnp.zeros((1, LANES), jnp.int32)
        at = 0
        for start, number in runs:

            def day(i, numbers, start=start, at=at, slot=slot, out_ref=out_ref, small=small):
                gram = jnp.zeros((width, width), jnp.float32)
                total = jnp.zeros((1, width), jnp.float32)
                for g, copy in enumerate(copies(start + i, slot + i)):
                    copy.wait()
                    count = counts_ref[0, g, start + i]
                    numbers += jnp.where(lane == at + i, count, 0)
                    block = held[slot + i, g]
                    left = jnp.concatenate([block.T, jnp.ones(rank.shape, block.dtype)], axis=0)
                    left = jnp.where(rank[:1] < count, left, jnp.zeros_like(left))
                    product = jnp.dot(left, block, preferred_element_type=jnp.float32)
                    gram += product[:width]
                    total += product[width : width + 1]
                base = pl.multiple_of((at + i) * FULL, FULL)
                low, diagonal_low = pack_quadrant(gram[:LANES, :LANES])
                high, diagonal_high = pack_quadrant(gram[LANES:, LANES:])
                out_ref[pl.ds(base, LANES)] = gram[:LANES, LANES:]
                out_ref[pl.ds(base + LANES, BLOCK)] = low
                out_ref[pl.ds(base + LANES + BLOCK, BLOCK)] = high
                row = small + SMALL * (at + i)
                out_ref[pl.ds(row, 1)] = diagonal_high + swap(diagonal_low)
                out_ref[pl.ds(row + 1, 1)] = total[:, :LANES]
                out_ref[pl.ds(row + 2, 1)] = total[:, LANES:]
                return numbers

            numbers = lax.fori_loop(0, number, day, numbers)
            at += number
            slot += number
        last = small + SMALL * days
        out_ref[last : last + 1] = numbers.astype(jnp.float32)


def gram(samples, counts, parts, after):
    _, groups, slots, width = samples.shape
    days = sum(length(runs) for runs in parts)
    rows = [length(runs) * FULL + small_rows(length(runs)) for runs in parts]
    outs, token = call(
        functools.partial(gram_kernel, parts),
        (counts, samples, after),
        (SCALARS, ANYWHERE, ANYWHERE),
        [(size, LANES) for size in rows],
        [
            pltpu.VMEM((days, groups, slots, width), samples.dtype),
            pltpu.SemaphoreType.DMA((days, groups)),
        ],
        2 * days * groups * slots * width * width,
        2 * days * groups * slots * width + 4 * sum(rows) * LANES,
        44,
    )
    return outs, token


def inner_kernel(days, year_ref, mine_ref, came_ref, after_ref, send_ref, keep_ref, token_ref):
    low_half = year_ref[0] < 2
    token_ref[...] = jnp.zeros_like(token_ref)

    def day(i, carry):
        src = pl.multiple_of(i * FULL, FULL)
        dst = pl.multiple_of(i * CROSS, CROSS)
        own = pl.multiple_of(i * BLOCK, BLOCK)
        q = pl.ds(src, LANES)
        send_ref[pl.ds(dst, LANES)] = mine_ref[q] + came_ref[q]
        low = pl.ds(src + LANES, BLOCK)
        high = pl.ds(src + LANES + BLOCK, BLOCK)
        low_sum = mine_ref[low] + came_ref[low]
        high_sum = mine_ref[high] + came_ref[high]
        send_ref[pl.ds(dst + LANES, BLOCK)] = jnp.where(low_half, high_sum, low_sum)
        keep_ref[pl.ds(own, BLOCK)] = jnp.where(low_half, low_sum, high_sum)
        return carry

    lax.fori_loop(0, days, day, 0)
    send_ref[days * CROSS :] = mine_ref[days * FULL :] + came_ref[days * FULL :]


def inner(year, mine, came, days, after):
    rows = days * CROSS + small_rows(days)
    (send, keep), token = call(
        functools.partial(inner_kernel, days),
        (year, mine, came, after),
        (SCALARS, INSIDE, INSIDE, ANYWHERE),
        [(rows, LANES), (days * BLOCK, LANES)],
        [],
        days * FULL * LANES,
        3 * 4 * days * FULL * LANES,
    )
    return send, keep, token


def cross_kernel(days, year_ref, mine_ref, keep_ref, came_ref, after_ref, send_ref, own_ref, token_ref):
    low_half = year_ref[0] < 2
    token_ref[...] = jnp.zeros_like(token_ref)
    _, lane = iotas((BLOCK, LANES))

    def day(i, carry):
        src = pl.multiple_of(i * CROSS, CROSS)
        own = pl.multiple_of(i * BLOCK, BLOCK)
        dst = pl.multiple_of(i * OWN, OWN)
        top = mine_ref[pl.ds(src, BLOCK)] + came_ref[pl.ds(src, BLOCK)]
        bottom = mine_ref[pl.ds(src + BLOCK, BLOCK)] + came_ref[pl.ds(src + BLOCK, BLOCK)]
        packed = keep_ref[pl.ds(own, BLOCK)] + came_ref[pl.ds(src + LANES, BLOCK)]
        first = jnp.where(lane < BLOCK, top, swap(bottom))
        second = jnp.where(lane < BLOCK, swap(top), bottom)
        send_ref[pl.ds(dst, BLOCK)] = packed
        own_ref[pl.ds(dst, BLOCK)] = packed
        send_ref[pl.ds(dst + BLOCK, BLOCK)] = jnp.where(low_half, top, second)
        own_ref[pl.ds(dst + BLOCK, BLOCK)] = jnp.where(low_half, bottom, first)
        return carry

    lax.fori_loop(0, days, day, 0)
    small = mine_ref[days * CROSS :] + came_ref[days * CROSS :]
    send_ref[days * OWN :] = small
    own_ref[days * OWN :] = small


def cross(year, mine, keep, came, days, after):
    rows = days * OWN + small_rows(days)
    (send, own), token = call(
        functools.partial(cross_kernel, days),
        (year, mine, keep, came, after),
        (SCALARS, INSIDE, INSIDE, INSIDE, ANYWHERE),
        [(rows, LANES)] * 2,
        [],
        days * CROSS * LANES,
        3 * 4 * days * CROSS * LANES,
    )
    return send, own, token


def is_outer(year):
    return (year == 0) | (year == 3)


def pick_kernel(runs, year_ref, own_ref, came_ref, after_ref, *refs):
    outs, token_ref = refs[:-1], refs[-1]
    outer = is_outer(year_ref[0])
    token_ref[...] = jnp.zeros_like(token_ref)

    def pick(start, size):
        return jnp.where(outer, came_ref[start : start + size], own_ref[start : start + size])

    small = length(runs) * OWN
    at = 0
    for (_, number), out_ref in zip(runs, outs):
        out_ref[: number * OWN] = pick(at * OWN, number * OWN)
        row = number * OWN
        out_ref[row : row + SMALL * number] = pick(small + SMALL * at, SMALL * number)
        counts = pick(small + SMALL * length(runs), 1)
        row += SMALL * number
        out_ref[row : row + 1] = pltpu.roll(counts, (LANES - at) % LANES, 1)
        at += number


def pick(year, own, came, runs, after):
    return call(
        functools.partial(pick_kernel, runs),
        (year, own, came, after),
        (SCALARS, INSIDE, INSIDE, ANYWHERE),
        [(size * OWN + small_rows(size), LANES) for _, size in runs],
        [],
        0,
        2 * 4 * own.size,
    )


def unpack(year, rows, diagonal):
    odd = lax.rem(year, 2) == 1
    low_half = year < 2
    row, lane = iotas((BLOCK, LANES))
    turned = rows.T
    top, bottom = rows[:BLOCK], rows[BLOCK:]
    top_turned, bottom_turned = turned[:BLOCK], turned[BLOCK:]
    upper = jnp.where(lane < BLOCK, jnp.where(row <= lane, top, top_turned), top)
    lower = swap(jnp.where(row > lane, top, top_turned))
    diagonal = jnp.where(low_half, diagonal, swap(diagonal))
    lower = jnp.where(row == lane - BLOCK, diagonal, lower)
    lower = jnp.where(lane < BLOCK, bottom_turned, lower)
    packed = jnp.where(odd, lower, upper)
    across = jnp.where(lane < BLOCK, swap(top_turned), bottom_turned)
    return jnp.where(low_half, packed, across), jnp.where(low_half, bottom, packed)


def windows_kernel(places, days, year_ref, *refs):
    parts = refs[: len(places)]
    win_ref, small_ref, token_ref, packed_ref = refs[len(places) + 1 :]
    token_ref[...] = jnp.zeros_like(token_ref)
    year = year_ref[0]
    extended = days + 2 * HALF
    where = {}
    for (place, number), ref in zip(places, parts):
        for i in range(number):
            where[place + i] = (ref, i, number * OWN)

    def sums(load, store):
        def add(a, b):
            return b if a is None else a if b is None else a + b

        def level(table, hop):
            return [add(table[k], table[k + hop]) for k in range(len(table) - hop)]

        ones = [load(*where[k]) if k in where else None for k in range(extended)]
        twos = level(ones, 1)
        fours = level(twos, 2)
        eights = level(fours, 4)
        for d in range(days):
            store(d, add(add(eights[d], fours[d + 8]), add(twos[d + 12], ones[d + 14])))

    def strip(s, carry):
        at = pl.multiple_of(s * SUBLANES, SUBLANES)

        def store(d, value):
            packed_ref[d, pl.ds(at, SUBLANES)] = value

        sums(lambda ref, i, small: ref[pl.ds(i * OWN + at, SUBLANES)], store)
        return carry

    lax.fori_loop(0, OWN // SUBLANES, strip, 0)

    for row in range(SMALL):

        def store_row(d, value):
            small_ref[row, d : d + 1] = value

        sums(lambda ref, i, small: ref[small + SMALL * i + row : small + SMALL * i + row + 1], store_row)

    lane = lax.broadcasted_iota(jnp.int32, (1, LANES), 1)

    def load_count(ref, i, small):
        last = small + SMALL * (small // OWN)
        count = jnp.sum(jnp.where(lane == i, ref[last : last + 1], 0.0), axis=1, keepdims=True)
        return jnp.broadcast_to(count, (1, LANES))

    def store_count(d, value):
        small_ref[SMALL, d : d + 1] = value

    sums(load_count, store_count)

    def day(d, carry):
        left, right = unpack(year, packed_ref[d], small_ref[0, pl.ds(d, 1)])
        win_ref[d, :, :LANES] = left
        win_ref[d, :, LANES:] = right
        return carry

    lax.fori_loop(0, days, day, 0)


def windows(year, parts, places, days, after):
    (win, small), token = call(
        functools.partial(windows_kernel, places, days),
        (year, *parts, after),
        [SCALARS] + [INSIDE] * len(parts) + [ANYWHERE],
        [(days, BLOCK, 2 * LANES), (SMALL + 1, days, LANES)],
        [pltpu.VMEM((days, OWN, LANES), jnp.float32)],
        6 * days * BLOCK * 2 * LANES,
        8 * days * BLOCK * 2 * LANES,
    )
    return win, small, token


def finish_kernel(places, pieces, year_ref, win_ref, small_ref, *refs):
    pairs, (after_ref, cov_ref, mean_ref, token_ref, formed, sent) = refs[: 2 * len(places)], refs[2 * len(places) :]
    token_ref[...] = jnp.zeros_like(token_ref)
    year = year_ref[0]
    outer = is_outer(year)
    days = win_ref.shape[0]
    lane = lax.broadcasted_iota(jnp.int32, (1, LANES), 1)
    day_of = lax.broadcasted_iota(jnp.int32, (days, LANES), 0)
    low, high, count = small_ref[1], small_ref[2], small_ref[SMALL]
    extras = []
    for p, (place, number) in enumerate(places):
        own_ref, came_ref = pairs[2 * p : 2 * p + 2]

        def pick(start, size):
            return jnp.where(outer, came_ref[start : start + size], own_ref[start : start + size])

        small = number * OWN
        numbers = pick(small + SMALL * number, 1)
        for i in range(number):
            inside = jnp.abs(day_of - (place + i)) <= HALF
            low += jnp.where(inside, pick(small + SMALL * i + 1, 1), 0.0)
            high += jnp.where(inside, pick(small + SMALL * i + 2, 1), 0.0)
            extra = jnp.sum(jnp.where(lane == i, numbers, 0.0), axis=1, keepdims=True)
            count += jnp.where(inside, extra, 0.0)
            extras.append((place + i, unpack(year, pick(i * OWN, OWN), pick(small + SMALL * i, 1))))
    low = low / count
    high = high / count
    own = jnp.where(year < 2, low, high)
    own = jnp.where(lax.rem(year, 2) == 1, swap(own), own)
    mean_ref[:, 0] = own[:, :BLOCK]
    turned = jnp.concatenate([own, jnp.zeros((LANES - days, LANES), jnp.float32)], axis=0).T
    scale = 1.0 / (count - 1.0)
    low = low * (count * scale)
    high = high * (count * scale)
    copies = []
    for first, size in pieces:
        for d in range(first, first + size):
            left, right = win_ref[d, :, :LANES], win_ref[d, :, LANES:]
            for at, (more_left, more_right) in extras:
                if abs(d - at) <= HALF:
                    left, right = left + more_left, right + more_right
            column = turned[:BLOCK, d : d + 1]
            factor = scale[d : d + 1]
            formed[d, :, :LANES] = left * factor - column * low[d : d + 1]
            formed[d, :, LANES:] = right * factor - column * high[d : d + 1]
        piece = pl.ds(first, size)
        copy = pltpu.make_async_copy(formed.at[piece], cov_ref.at[0, piece], sent.at[len(copies)])
        copy.start()
        copies.append(copy)
    for copy in copies:
        copy.wait()


def finish(year, win, small, pairs, places, after):
    days, _, width = win.shape
    size = -(-days // 3)
    pieces = tuple((first, min(size, days - first)) for first in range(0, days, size))
    flat = [array for pair in pairs for array in pair]
    (covariance, mean), _ = call(
        functools.partial(finish_kernel, places, pieces),
        (year, win, small, *flat, after),
        [SCALARS] + [INSIDE] * (2 + len(flat)) + [ANYWHERE],
        [(1, days, BLOCK, width), (days, 1, BLOCK)],
        [pltpu.VMEM((days, BLOCK, width), jnp.float32), pltpu.SemaphoreType.DMA((len(pieces),))],
        6 * days * BLOCK * width,
        8 * days * BLOCK * width,
        outs=[ANYWHERE, INSIDE],
    )
    return covariance, mean


def plan(days):
    near = min(5, HALF)
    rest = HALF - near
    parts = [((0, near),), ((days - near, near),), ((near, rest), (days - HALF, rest))]
    at, left = HALF, days - 2 * HALF
    for size in (left - 5, 3, 2):
        parts.append(((at, size),))
        at += size
    return parts


def shards(samples, counts):
    days = samples.shape[0]
    day_size = lax.axis_size("day")
    position = lax.axis_index("year")
    year = position.astype(jnp.int32)[None]
    inward = [(0, 1), (3, 2)]
    between = [(1, 2), (2, 1)]
    outward = [(1, 0), (2, 3)]
    right = [(i, (i + 1) % day_size) for i in range(day_size)]
    left = [((i + 1) % day_size, i) for i in range(day_size)]
    counts = jnp.transpose(counts, (0, 2, 1))
    parts = plan(days)
    token = jnp.zeros(TOKEN, jnp.float32)
    mine, sums, rows = {}, {}, {}
    totals, places = [], []

    def gram_step(*ks):
        nonlocal token
        outs, token = gram(samples, counts, tuple(parts[k] for k in ks), token)
        for k, out in zip(ks, outs):
            mine[k] = (out, lax.ppermute(out, "year", inward))

    def inner_step(k):
        nonlocal token
        send, keep, token = inner(year, *mine[k], length(parts[k]), token)
        sums[k] = (send, keep, lax.ppermute(send, "year", between))

    def cross_step(k):
        nonlocal token
        send, own, token = cross(year, *sums[k], length(parts[k]), token)
        rows[k] = (own, lax.ppermute(send, "year", outward))

    def pick_step(k):
        nonlocal token
        outs, token = pick(year, *rows[k], parts[k], token)
        for (start, size), out in zip(parts[k], outs):
            totals.append(out)
            places.append((start + HALF, size))
            if start < HALF:
                totals.append(lax.ppermute(out, "day", left))
                places.append((start + HALF + days, size))
            elif start >= days - HALF:
                totals.append(lax.ppermute(out, "day", right))
                places.append((start + HALF - days, size))

    gram_step(0)
    gram_step(1, 2)
    inner_step(0)
    gram_step(3, 4, 5)
    inner_step(1)
    cross_step(0)
    inner_step(2)
    pick_step(0)
    cross_step(1)
    inner_step(3)
    pick_step(1)
    cross_step(2)
    inner_step(4)
    pick_step(2)
    cross_step(3)
    inner_step(5)
    cross_step(4)
    pick_step(3)
    win, small, token = windows(year, totals, tuple(places), days, token)
    cross_step(5)
    last = tuple((parts[k][0][0], parts[k][0][1]) for k in (4, 5))
    covariance, mean = finish(year, win, small, (rows[4], rows[5]), last, token)
    return covariance, jnp.transpose(mean, (1, 0, 2))


def solution(mesh):
    placed = (P("day", "year", "region", None), P("region", "day", "year"))
    return jax.shard_map(
        shards,
        mesh=mesh,
        in_specs=placed,
        out_specs=(P("region", "day", "year", None), P("region", "day", "year")),
        check_vma=False,
    )
```

```python
import functools

import jax
import jax.numpy as jnp
from jax import lax
from jax.experimental import pallas as pl
from jax.experimental.pallas import tpu as pltpu
from jax.sharding import PartitionSpec as P

HALF = 7
LANES = 128
BLOCK = 64
SUBLANES = 8
FULL, CROSS, OWN = 4 * BLOCK, 3 * BLOCK, 2 * BLOCK
SMALL = 3
TOKEN = (SUBLANES, LANES)
SCALARS = pl.BlockSpec(memory_space=pltpu.SMEM)
INSIDE = pl.BlockSpec(memory_space=pltpu.VMEM)
ANYWHERE = pl.BlockSpec(memory_space=pl.ANY)


def small_rows(days):
    return -(-(SMALL * days + 1) // SUBLANES) * SUBLANES


def length(runs):
    return sum(size for _, size in runs)


def call(kernel, args, specs, shapes, scratch, flops, moved, mebibytes=16, outs=None):
    results = pl.pallas_call(
        kernel,
        in_specs=list(specs),
        out_specs=(list(outs) if outs else [INSIDE] * len(shapes)) + [INSIDE],
        out_shape=[jax.ShapeDtypeStruct(shape, jnp.float32) for shape in list(shapes) + [TOKEN]],
        scratch_shapes=scratch,
        cost_estimate=pl.CostEstimate(flops=0, bytes_accessed=0, transcendentals=0),
        compiler_params=pltpu.CompilerParams(vmem_limit_bytes=mebibytes * 1024 * 1024),
    )(*args)
    return results[:-1], results[-1]


def iotas(shape):
    return lax.broadcasted_iota(jnp.int32, shape, 0), lax.broadcasted_iota(jnp.int32, shape, 1)


def swap(block):
    return pltpu.roll(block, BLOCK, 1)


def pack_quadrant(quadrant):
    top, bottom = quadrant[:BLOCK], swap(quadrant[BLOCK:])
    row, lane = iotas((BLOCK, LANES))
    packed = jnp.where((lane < BLOCK) & (row > lane), bottom, top)
    diagonal = jnp.sum(jnp.where(row == lane, bottom, 0.0), axis=0, keepdims=True)
    return packed, diagonal


def gram_kernel(parts, counts_ref, samples_ref, after_ref, *refs):
    outs, token_ref, held, arrived = refs[: len(parts)], *refs[len(parts) :]
    groups, slots, width = held.shape[1:]
    lane = lax.broadcasted_iota(jnp.int32, (1, LANES), 1)
    rank = lax.broadcasted_iota(jnp.int32, (1, slots), 1)
    token_ref[...] = jnp.zeros_like(token_ref)

    def copies(day, slot):
        return [
            pltpu.make_async_copy(samples_ref.at[day, g], held.at[slot, g], arrived.at[slot, g])
            for g in range(groups)
        ]

    slot = 0
    for runs in parts:
        for start, number in runs:
            for i in range(number):
                for copy in copies(start + i, slot + i):
                    copy.start()
            slot += number
    slot = 0
    for runs, out_ref in zip(parts, outs):
        days = length(runs)
        small = days * FULL
        out_ref[small:] = jnp.zeros((small_rows(days), LANES), jnp.float32)
        numbers = jnp.zeros((1, LANES), jnp.int32)
        at = 0
        for start, number in runs:

            def day(i, numbers, start=start, at=at, slot=slot, out_ref=out_ref, small=small):
                gram = jnp.zeros((width, width), jnp.float32)
                total = jnp.zeros((1, width), jnp.float32)
                for copy in copies(start + i, slot + i):
                    copy.wait()
                for g in range(groups):
                    count = counts_ref[0, g, start + i]
                    numbers += jnp.where(lane == at + i, count, 0)
                    block = held[slot + i, g]
                    left = jnp.concatenate([block.T, jnp.ones((2 * SUBLANES, slots), block.dtype)], axis=0)
                    left = jnp.where(rank < count, left, jnp.zeros_like(left))
                    product = jnp.dot(left, block, preferred_element_type=jnp.float32)
                    gram += product[:width]
                    total += product[width : width + 1]
                base = pl.multiple_of((at + i) * FULL, FULL)
                low, diagonal_low = pack_quadrant(gram[:LANES, :LANES])
                high, diagonal_high = pack_quadrant(gram[LANES:, LANES:])
                out_ref[pl.ds(base, LANES)] = gram[:LANES, LANES:]
                out_ref[pl.ds(base + LANES, BLOCK)] = low
                out_ref[pl.ds(base + LANES + BLOCK, BLOCK)] = high
                row = small + SMALL * (at + i)
                out_ref[pl.ds(row, 1)] = diagonal_high + swap(diagonal_low)
                out_ref[pl.ds(row + 1, 1)] = total[:, :LANES]
                out_ref[pl.ds(row + 2, 1)] = total[:, LANES:]
                return numbers

            numbers = lax.fori_loop(0, number, day, numbers)
            at += number
            slot += number
        last = small + SMALL * days
        out_ref[last : last + 1] = numbers.astype(jnp.float32)


def gram(samples, counts, parts, after):
    _, groups, slots, width = samples.shape
    days = sum(length(runs) for runs in parts)
    rows = [length(runs) * FULL + small_rows(length(runs)) for runs in parts]
    outs, token = call(
        functools.partial(gram_kernel, parts),
        (counts, samples, after),
        (SCALARS, ANYWHERE, ANYWHERE),
        [(size, LANES) for size in rows],
        [
            pltpu.VMEM((days, groups, slots, width), samples.dtype),
            pltpu.SemaphoreType.DMA((days, groups)),
        ],
        2 * days * groups * slots * width * width,
        2 * days * groups * slots * width + 4 * sum(rows) * LANES,
        44,
    )
    return outs, token


def inner_kernel(days, year_ref, mine_ref, came_ref, after_ref, send_ref, keep_ref, token_ref):
    low_half = year_ref[0] < 2
    token_ref[...] = jnp.zeros_like(token_ref)

    def day(i, carry):
        src = pl.multiple_of(i * FULL, FULL)
        dst = pl.multiple_of(i * CROSS, CROSS)
        own = pl.multiple_of(i * BLOCK, BLOCK)
        q = pl.ds(src, LANES)
        send_ref[pl.ds(dst, LANES)] = mine_ref[q] + came_ref[q]
        low = pl.ds(src + LANES, BLOCK)
        high = pl.ds(src + LANES + BLOCK, BLOCK)
        low_sum = mine_ref[low] + came_ref[low]
        high_sum = mine_ref[high] + came_ref[high]
        send_ref[pl.ds(dst + LANES, BLOCK)] = jnp.where(low_half, high_sum, low_sum)
        keep_ref[pl.ds(own, BLOCK)] = jnp.where(low_half, low_sum, high_sum)
        return carry

    lax.fori_loop(0, days, day, 0)
    send_ref[days * CROSS :] = mine_ref[days * FULL :] + came_ref[days * FULL :]


def inner(year, mine, came, days, after):
    rows = days * CROSS + small_rows(days)
    (send, keep), token = call(
        functools.partial(inner_kernel, days),
        (year, mine, came, after),
        (SCALARS, INSIDE, INSIDE, ANYWHERE),
        [(rows, LANES), (days * BLOCK, LANES)],
        [],
        days * FULL * LANES,
        3 * 4 * days * FULL * LANES,
    )
    return send, keep, token


def cross_kernel(days, year_ref, mine_ref, keep_ref, came_ref, after_ref, send_ref, own_ref, token_ref):
    low_half = year_ref[0] < 2
    token_ref[...] = jnp.zeros_like(token_ref)
    _, lane = iotas((BLOCK, LANES))

    def day(i, carry):
        src = pl.multiple_of(i * CROSS, CROSS)
        own = pl.multiple_of(i * BLOCK, BLOCK)
        dst = pl.multiple_of(i * OWN, OWN)
        top = mine_ref[pl.ds(src, BLOCK)] + came_ref[pl.ds(src, BLOCK)]
        bottom = mine_ref[pl.ds(src + BLOCK, BLOCK)] + came_ref[pl.ds(src + BLOCK, BLOCK)]
        packed = keep_ref[pl.ds(own, BLOCK)] + came_ref[pl.ds(src + LANES, BLOCK)]
        first = jnp.where(lane < BLOCK, top, swap(bottom))
        second = jnp.where(lane < BLOCK, swap(top), bottom)
        send_ref[pl.ds(dst, BLOCK)] = packed
        own_ref[pl.ds(dst, BLOCK)] = packed
        send_ref[pl.ds(dst + BLOCK, BLOCK)] = jnp.where(low_half, top, second)
        own_ref[pl.ds(dst + BLOCK, BLOCK)] = jnp.where(low_half, bottom, first)
        return carry

    lax.fori_loop(0, days, day, 0)
    small = mine_ref[days * CROSS :] + came_ref[days * CROSS :]
    send_ref[days * OWN :] = small
    own_ref[days * OWN :] = small


def cross(year, mine, keep, came, days, after):
    rows = days * OWN + small_rows(days)
    (send, own), token = call(
        functools.partial(cross_kernel, days),
        (year, mine, keep, came, after),
        (SCALARS, INSIDE, INSIDE, INSIDE, ANYWHERE),
        [(rows, LANES)] * 2,
        [],
        days * CROSS * LANES,
        3 * 4 * days * CROSS * LANES,
    )
    return send, own, token


def is_outer(year):
    return (year == 0) | (year == 3)


def pick_kernel(runs, year_ref, own_ref, came_ref, after_ref, *refs):
    outs, token_ref = refs[:-1], refs[-1]
    outer = is_outer(year_ref[0])
    token_ref[...] = jnp.zeros_like(token_ref)

    def pick(start, size):
        return jnp.where(outer, came_ref[start : start + size], own_ref[start : start + size])

    small = length(runs) * OWN
    at = 0
    for (_, number), out_ref in zip(runs, outs):
        out_ref[: number * OWN] = pick(at * OWN, number * OWN)
        row = number * OWN
        out_ref[row : row + SMALL * number] = pick(small + SMALL * at, SMALL * number)
        counts = pick(small + SMALL * length(runs), 1)
        row += SMALL * number
        out_ref[row : row + 1] = pltpu.roll(counts, (LANES - at) % LANES, 1)
        at += number


def pick(year, own, came, runs, after):
    return call(
        functools.partial(pick_kernel, runs),
        (year, own, came, after),
        (SCALARS, INSIDE, INSIDE, ANYWHERE),
        [(size * OWN + small_rows(size), LANES) for _, size in runs],
        [],
        0,
        2 * 4 * own.size,
    )


def unpack(year, rows, diagonal):
    odd = lax.rem(year, 2) == 1
    low_half = year < 2
    row, lane = iotas((BLOCK, LANES))
    turned = rows.T
    top, bottom = rows[:BLOCK], rows[BLOCK:]
    top_turned, bottom_turned = turned[:BLOCK], turned[BLOCK:]
    upper = jnp.where(lane < BLOCK, jnp.where(row <= lane, top, top_turned), top)
    lower = swap(jnp.where(row > lane, top, top_turned))
    diagonal = jnp.where(low_half, diagonal, swap(diagonal))
    lower = jnp.where(row == lane - BLOCK, diagonal, lower)
    lower = jnp.where(lane < BLOCK, bottom_turned, lower)
    packed = jnp.where(odd, lower, upper)
    across = jnp.where(lane < BLOCK, swap(top_turned), bottom_turned)
    return jnp.where(low_half, packed, across), jnp.where(low_half, bottom, packed)


def windows_kernel(places, days, year_ref, *refs):
    parts = refs[: len(places)]
    win_ref, small_ref, token_ref, packed_ref = refs[len(places) + 1 :]
    token_ref[...] = jnp.zeros_like(token_ref)
    year = year_ref[0]
    extended = days + 2 * HALF
    where = {}
    for (place, number), ref in zip(places, parts):
        for i in range(number):
            where[place + i] = (ref, i, number * OWN)

    def sums(load, store):
        def add(a, b):
            return b if a is None else a if b is None else a + b

        def level(table, hop):
            return [add(table[k], table[k + hop]) for k in range(len(table) - hop)]

        ones = [load(*where[k]) if k in where else None for k in range(extended)]
        twos = level(ones, 1)
        fours = level(twos, 2)
        eights = level(fours, 4)
        for d in range(days):
            store(d, add(add(eights[d], fours[d + 8]), add(twos[d + 12], ones[d + 14])))

    def strip(s, carry):
        at = pl.multiple_of(s * SUBLANES, SUBLANES)

        def store(d, value):
            packed_ref[d, pl.ds(at, SUBLANES)] = value

        sums(lambda ref, i, small: ref[pl.ds(i * OWN + at, SUBLANES)], store)
        return carry

    lax.fori_loop(0, OWN // SUBLANES, strip, 0)

    for row in range(SMALL):

        def store_row(d, value):
            small_ref[row, d : d + 1] = value

        sums(lambda ref, i, small: ref[small + SMALL * i + row : small + SMALL * i + row + 1], store_row)

    lane = lax.broadcasted_iota(jnp.int32, (1, LANES), 1)

    def load_count(ref, i, small):
        last = small + SMALL * (small // OWN)
        count = jnp.sum(jnp.where(lane == i, ref[last : last + 1], 0.0), axis=1, keepdims=True)
        return jnp.broadcast_to(count, (1, LANES))

    def store_count(d, value):
        small_ref[SMALL, d : d + 1] = value

    sums(load_count, store_count)

    def day(d, carry):
        left, right = unpack(year, packed_ref[d], small_ref[0, pl.ds(d, 1)])
        win_ref[d, :, :LANES] = left
        win_ref[d, :, LANES:] = right
        return carry

    lax.fori_loop(0, days, day, 0, unroll=True)


def windows(year, parts, places, days, after):
    (win, small), token = call(
        functools.partial(windows_kernel, places, days),
        (year, *parts, after),
        [SCALARS] + [INSIDE] * len(parts) + [ANYWHERE],
        [(days, BLOCK, 2 * LANES), (SMALL + 1, days, LANES)],
        [pltpu.VMEM((days, OWN, LANES), jnp.float32)],
        6 * days * BLOCK * 2 * LANES,
        8 * days * BLOCK * 2 * LANES,
    )
    return win, small, token


def finish_kernel(places, pieces, year_ref, win_ref, small_ref, *refs):
    pairs, (after_ref, cov_ref, mean_ref, token_ref, formed, sent) = refs[: 2 * len(places)], refs[2 * len(places) :]
    token_ref[...] = jnp.zeros_like(token_ref)
    year = year_ref[0]
    outer = is_outer(year)
    days = win_ref.shape[0]
    lane = lax.broadcasted_iota(jnp.int32, (1, LANES), 1)
    day_of = lax.broadcasted_iota(jnp.int32, (days, LANES), 0)
    low, high, count = small_ref[1], small_ref[2], small_ref[SMALL]
    extras = []
    for p, (place, number) in enumerate(places):
        own_ref, came_ref = pairs[2 * p : 2 * p + 2]

        def pick(start, size):
            return jnp.where(outer, came_ref[start : start + size], own_ref[start : start + size])

        small = number * OWN
        numbers = pick(small + SMALL * number, 1)
        for i in range(number):
            inside = jnp.abs(day_of - (place + i)) <= HALF
            low += jnp.where(inside, pick(small + SMALL * i + 1, 1), 0.0)
            high += jnp.where(inside, pick(small + SMALL * i + 2, 1), 0.0)
            extra = jnp.sum(jnp.where(lane == i, numbers, 0.0), axis=1, keepdims=True)
            count += jnp.where(inside, extra, 0.0)
            extras.append((place + i, unpack(year, pick(i * OWN, OWN), pick(small + SMALL * i, 1))))
    low = low / count
    high = high / count
    own = jnp.where(year < 2, low, high)
    own = jnp.where(lax.rem(year, 2) == 1, swap(own), own)
    mean_ref[:, 0] = own[:, :BLOCK]
    turned = jnp.concatenate([own, jnp.zeros((LANES - days, LANES), jnp.float32)], axis=0).T
    scale = 1.0 / (count - 1.0)
    low = low * (count * scale)
    high = high * (count * scale)
    copies = []
    for first, size in pieces:
        for d in range(first, first + size):
            left, right = win_ref[d, :, :LANES], win_ref[d, :, LANES:]
            for at, (more_left, more_right) in extras:
                if abs(d - at) <= HALF:
                    left, right = left + more_left, right + more_right
            column = turned[:BLOCK, d : d + 1]
            factor = scale[d : d + 1]
            formed[d, :, :LANES] = left * factor - column * low[d : d + 1]
            formed[d, :, LANES:] = right * factor - column * high[d : d + 1]
        piece = pl.ds(first, size)
        copy = pltpu.make_async_copy(formed.at[piece], cov_ref.at[0, piece], sent.at[len(copies)])
        copy.start()
        copies.append(copy)
    for copy in copies:
        copy.wait()


def finish(year, win, small, pairs, places, after):
    days, _, width = win.shape
    size = -(-days // 3)
    pieces = tuple((first, min(size, days - first)) for first in range(0, days, size))
    flat = [array for pair in pairs for array in pair]
    (covariance, mean), _ = call(
        functools.partial(finish_kernel, places, pieces),
        (year, win, small, *flat, after),
        [SCALARS] + [INSIDE] * (2 + len(flat)) + [ANYWHERE],
        [(1, days, BLOCK, width), (days, 1, BLOCK)],
        [pltpu.VMEM((days, BLOCK, width), jnp.float32), pltpu.SemaphoreType.DMA((len(pieces),))],
        6 * days * BLOCK * width,
        8 * days * BLOCK * width,
        outs=[ANYWHERE, INSIDE],
    )
    return covariance, mean


def plan(days):
    parts = [((0, 4),), ((days - 5, 5),), ((4, HALF - 4), (days - HALF, HALF - 5))]
    at, left = HALF, days - 2 * HALF
    for size in (left - 5, 3, 2):
        parts.append(((at, size),))
        at += size
    return parts


ORDER = (
    ("gram", 0),
    ("gram", 1),
    ("gram", 2, 3, 4, 5),
    ("inner", 0),
    ("inner", 1),
    ("cross", 0),
    ("inner", 2),
    ("pick", 0),
    ("cross", 1),
    ("inner", 3),
    ("pick", 1),
    ("cross", 2),
    ("inner", 4),
    ("cross", 3),
    ("inner", 5),
    ("pick", 2),
    ("cross", 4),
    ("pick", 3),
    ("cross", 5),
    ("windows",),
    ("finish", 4, 5),
)


def shards(samples, counts):
    days = samples.shape[0]
    day_size = lax.axis_size("day")
    position = lax.axis_index("year")
    year = position.astype(jnp.int32)[None]
    inward = [(0, 1), (3, 2)]
    between = [(1, 2), (2, 1)]
    outward = [(1, 0), (2, 3)]
    right = [(i, (i + 1) % day_size) for i in range(day_size)]
    left = [((i + 1) % day_size, i) for i in range(day_size)]
    counts = jnp.transpose(counts, (0, 2, 1))
    parts = plan(days)
    token = jnp.zeros(TOKEN, jnp.float32)
    mine, sums, rows = {}, {}, {}
    totals, places = [], []

    def gram_step(*ks):
        nonlocal token
        outs, token = gram(samples, counts, tuple(parts[k] for k in ks), token)
        for k, out in zip(ks, outs):
            mine[k] = (out, lax.ppermute(out, "year", inward))

    def inner_step(k):
        nonlocal token
        send, keep, token = inner(year, *mine[k], length(parts[k]), token)
        sums[k] = (send, keep, lax.ppermute(send, "year", between))

    def cross_step(k):
        nonlocal token
        send, own, token = cross(year, *sums[k], length(parts[k]), token)
        rows[k] = (own, lax.ppermute(send, "year", outward))

    def pick_step(k):
        nonlocal token
        outs, token = pick(year, *rows[k], parts[k], token)
        for (start, size), out in zip(parts[k], outs):
            totals.append(out)
            places.append((start + HALF, size))
            if start < HALF:
                totals.append(lax.ppermute(out, "day", left))
                places.append((start + HALF + days, size))
            elif start >= days - HALF:
                totals.append(lax.ppermute(out, "day", right))
                places.append((start + HALF - days, size))

    def windows_step():
        nonlocal token
        win, small, token = windows(year, totals, tuple(places), days, token)
        return win, small

    def finish_step(*ks):
        last = tuple(parts[k][0] for k in ks)
        return finish(year, *held, [rows[k] for k in ks], last, token)

    steps = {
        "gram": gram_step,
        "inner": inner_step,
        "cross": cross_step,
        "pick": pick_step,
        "windows": windows_step,
        "finish": finish_step,
    }
    held = None
    for name, *ks in ORDER:
        result = steps[name](*ks)
        held = result if result else held
    covariance, mean = held
    return covariance, jnp.transpose(mean, (1, 0, 2))


def solution(mesh):
    placed = (P("day", "year", "region", None), P("region", "day", "year"))
    return jax.shard_map(
        shards,
        mesh=mesh,
        in_specs=placed,
        out_specs=(P("region", "day", "year", None), P("region", "day", "year")),
        check_vma=False,
    )
```

```python
import functools

import jax
import jax.numpy as jnp
from jax import lax
from jax.experimental import pallas as pl
from jax.experimental.pallas import tpu as pltpu
from jax.sharding import PartitionSpec as P

HALF = 7
LANES = 128
BLOCK = 64
SUBLANES = 8
FULL, CROSS, OWN = 4 * BLOCK, 3 * BLOCK, 2 * BLOCK
PAIR = BLOCK + BLOCK // 2
SMALL = 3
TOKEN = (SUBLANES, LANES)
SCALARS = pl.BlockSpec(memory_space=pltpu.SMEM)
INSIDE = pl.BlockSpec(memory_space=pltpu.VMEM)
ANYWHERE = pl.BlockSpec(memory_space=pl.ANY)


def small_rows(days):
    return -(-(SMALL * days + 1) // SUBLANES) * SUBLANES


def length(runs):
    return sum(size for _, size in runs)


def call(kernel, args, specs, shapes, scratch, flops, moved, mebibytes=16, outs=None):
    *args, (after, *others) = args
    results = pl.pallas_call(
        lambda *refs: kernel(*refs[len(others) :]),
        in_specs=[ANYWHERE] * len(others) + list(specs),
        out_specs=(list(outs) if outs else [INSIDE] * len(shapes)) + [INSIDE],
        out_shape=[jax.ShapeDtypeStruct(shape, jnp.float32) for shape in list(shapes) + [TOKEN]],
        scratch_shapes=scratch,
        cost_estimate=pl.CostEstimate(flops=0, bytes_accessed=0, transcendentals=0),
        compiler_params=pltpu.CompilerParams(vmem_limit_bytes=mebibytes * 1024 * 1024),
    )(*others, *args, after)
    return results[:-1], results[-1:]


def sent_rows(days):
    return days * CROSS + days // 2 * PAIR + days % 2 * BLOCK


def iotas(shape):
    return lax.broadcasted_iota(jnp.int32, shape, 0), lax.broadcasted_iota(jnp.int32, shape, 1)


def swap(block):
    return pltpu.roll(block, BLOCK, 1)


def pack_quadrant(quadrant):
    top, bottom = quadrant[:BLOCK], swap(quadrant[BLOCK:])
    row, lane = iotas((BLOCK, LANES))
    packed = jnp.where((lane < BLOCK) & (row > lane), bottom, top)
    diagonal = jnp.sum(jnp.where(row == lane, bottom, 0.0), axis=0, keepdims=True)
    return packed, diagonal


def own_side(row, lane, low_half):
    ahead = jnp.where(low_half, lane - row, row - lane - 1)
    return (lane < BLOCK) & (ahead >= 0)


def half_rows(ref, i, low_half):
    return ref[pl.ds(pl.multiple_of(i * FULL + LANES + jnp.where(low_half, 0, BLOCK), BLOCK), BLOCK)]


def pack_sent(days, low_half, mine_ref, sent_ref):
    row, lane = iotas((BLOCK, LANES))
    own = own_side(row, lane, low_half)
    small, at = days * FULL, sent_rows(days)
    sent_ref[at:] = mine_ref[small:]

    def day(i, carry):
        src = pl.multiple_of(i * FULL, FULL)
        dst = pl.multiple_of(i * CROSS, CROSS)
        sent_ref[pl.ds(dst, LANES)] = mine_ref[pl.ds(src, LANES)]
        sent_ref[pl.ds(dst + LANES, BLOCK)] = half_rows(mine_ref, i, ~low_half)
        diagonal = jnp.sum(jnp.where(row == lane, half_rows(mine_ref, i, low_half), 0.0), axis=0, keepdims=True)
        kept = mine_ref[pl.ds(small + SMALL * i, 1)]
        sent_ref[pl.ds(at + SMALL * i, 1)] = jnp.where(low_half | (lane[:1] >= BLOCK), kept, diagonal)
        return carry

    lax.fori_loop(0, days, day, 0)

    def pair(p, carry):
        first, second = half_rows(mine_ref, 2 * p, low_half), half_rows(mine_ref, 2 * p + 1, low_half)
        turned = jnp.concatenate([first, second], axis=0).T[:BLOCK]
        below = jnp.where(low_half, first, turned)
        above = jnp.where(low_half, swap(turned), second)
        triangles = jnp.where(row > lane, below, above)
        dst = pl.multiple_of(days * CROSS + p * PAIR, PAIR // 3)
        sent_ref[pl.ds(dst, BLOCK)] = jnp.where(lane < BLOCK, swap(first), second)
        rest = jnp.where(lane[: BLOCK // 2] < BLOCK, triangles[: BLOCK // 2], swap(triangles[BLOCK // 2 :]))
        sent_ref[pl.ds(dst + BLOCK, BLOCK // 2)] = rest
        return carry

    lax.fori_loop(0, days // 2, pair, 0)
    if days % 2:
        last = days * CROSS + days // 2 * PAIR
        sent_ref[last : last + BLOCK] = jnp.where(own, 0.0, half_rows(mine_ref, days - 1, low_half))


def gram_kernel(parts, counts_ref, year_ref, samples_ref, after_ref, *refs):
    outs, sents = refs[: len(parts)], refs[len(parts) : 2 * len(parts)]
    token_ref, held, arrived = refs[2 * len(parts) :]
    low_half = year_ref[0] < 2
    groups, slots, width = held.shape[1:]
    lane = lax.broadcasted_iota(jnp.int32, (1, LANES), 1)
    rank = lax.broadcasted_iota(jnp.int32, (1, slots), 1)
    token_ref[...] = jnp.zeros_like(token_ref)

    def copies(day, slot):
        return [
            pltpu.make_async_copy(samples_ref.at[day, g], held.at[slot, g], arrived.at[slot, g])
            for g in range(groups)
        ]

    slot = 0
    for runs in parts:
        for start, number in runs:
            for i in range(number):
                for copy in copies(start + i, slot + i):
                    copy.start()
            slot += number
    slot = 0
    for runs, out_ref, sent_ref in zip(parts, outs, sents):
        days = length(runs)
        small = days * FULL
        out_ref[small:] = jnp.zeros((small_rows(days), LANES), jnp.float32)
        numbers = jnp.zeros((1, LANES), jnp.int32)
        at = 0
        for start, number in runs:

            def day(i, numbers, start=start, at=at, slot=slot, out_ref=out_ref, small=small):
                gram = jnp.zeros((width, width), jnp.float32)
                total = jnp.zeros((1, width), jnp.float32)
                for copy in copies(start + i, slot + i):
                    copy.wait()
                for g in range(groups):
                    count = counts_ref[0, g, start + i]
                    numbers += jnp.where(lane == at + i, count, 0)
                    block = held[slot + i, g]
                    left = jnp.concatenate([block.T, jnp.ones((2 * SUBLANES, slots), block.dtype)], axis=0)
                    left = jnp.where(rank < count, left, jnp.zeros_like(left))
                    product = jnp.dot(left, block, preferred_element_type=jnp.float32)
                    gram += product[:width]
                    total += product[width : width + 1]
                base = pl.multiple_of((at + i) * FULL, FULL)
                low, diagonal_low = pack_quadrant(gram[:LANES, :LANES])
                high, diagonal_high = pack_quadrant(gram[LANES:, LANES:])
                out_ref[pl.ds(base, LANES)] = gram[:LANES, LANES:]
                out_ref[pl.ds(base + LANES, BLOCK)] = low
                out_ref[pl.ds(base + LANES + BLOCK, BLOCK)] = high
                row = small + SMALL * (at + i)
                out_ref[pl.ds(row, 1)] = diagonal_high + swap(diagonal_low)
                out_ref[pl.ds(row + 1, 1)] = total[:, :LANES]
                out_ref[pl.ds(row + 2, 1)] = total[:, LANES:]
                return numbers

            numbers = lax.fori_loop(0, number, day, numbers)
            at += number
            slot += number
        last = small + SMALL * days
        out_ref[last : last + 1] = numbers.astype(jnp.float32)
        pack_sent(days, low_half, out_ref, sent_ref)


def gram(samples, counts, year, parts, after):
    _, groups, slots, width = samples.shape
    days = sum(length(runs) for runs in parts)
    rows = [length(runs) * FULL + small_rows(length(runs)) for runs in parts]
    rows += [sent_rows(length(runs)) + small_rows(length(runs)) for runs in parts]
    outs, token = call(
        functools.partial(gram_kernel, parts),
        (counts, year, samples, after),
        (SCALARS, SCALARS, ANYWHERE, ANYWHERE),
        [(size, LANES) for size in rows],
        [
            pltpu.VMEM((days, groups, slots, width), samples.dtype),
            pltpu.SemaphoreType.DMA((days, groups)),
        ],
        2 * days * groups * slots * width * width,
        2 * days * groups * slots * width + 4 * sum(rows) * LANES,
        44,
    )
    return list(zip(outs[: len(parts)], outs[len(parts) :])), token


def inner_kernel(days, year_ref, mine_ref, came_ref, after_ref, send_ref, keep_ref, token_ref):
    low_half = year_ref[0] < 2
    token_ref[...] = jnp.zeros_like(token_ref)
    row, lane = iotas((BLOCK, LANES))
    at = sent_rows(days)

    def day(i, carry):
        src = pl.multiple_of(i * FULL, FULL)
        dst = pl.multiple_of(i * CROSS, CROSS)
        send_ref[pl.ds(dst, LANES)] = mine_ref[pl.ds(src, LANES)] + came_ref[pl.ds(dst, LANES)]
        other = pl.ds(dst + LANES, BLOCK)
        send_ref[other] = half_rows(mine_ref, i, ~low_half) + came_ref[other]
        return carry

    lax.fori_loop(0, days, day, 0)

    def pair(p, carry):
        src = pl.multiple_of(days * CROSS + p * PAIR, PAIR // 3)
        blocks = came_ref[pl.ds(src, BLOCK)]
        rest = came_ref[pl.ds(src + BLOCK, BLOCK // 2)]
        triangles = jnp.concatenate([rest, swap(rest)], axis=0)
        turned = jnp.concatenate([triangles, jnp.zeros_like(triangles)], axis=0).T[:BLOCK]
        side = jnp.where(low_half, row - lane, lane - row)
        for k, block in enumerate((swap(blocks), blocks)):
            i = 2 * p + k
            triangle = jnp.where(low_half, (triangles, turned)[k], (turned, triangles)[k])
            diagonal = jnp.where(low_half, 0.0, came_ref[pl.ds(at + SMALL * i, 1)])
            triangle = jnp.where(side > 0, triangle, jnp.where(side == 0, diagonal, 0.0))
            keep_ref[pl.ds(pl.multiple_of(i * BLOCK, BLOCK), BLOCK)] = half_rows(mine_ref, i, low_half) + jnp.where(
                lane < BLOCK, triangle, block
            )
        return carry

    lax.fori_loop(0, days // 2, pair, 0)
    if days % 2:
        last = at - BLOCK
        keep_ref[(days - 1) * BLOCK :] = half_rows(mine_ref, days - 1, low_half) + came_ref[last:at]
    row, lane = iotas((small_rows(days), LANES))
    diagonals = (lax.rem(row, SMALL) == 0) & (row < SMALL * days) & (lane < BLOCK)
    came = jnp.where(diagonals & ~low_half, 0.0, came_ref[at:])
    send_ref[days * CROSS :] = mine_ref[days * FULL :] + came


def inner(year, mine, came, days, after):
    rows = days * CROSS + small_rows(days)
    (send, keep), token = call(
        functools.partial(inner_kernel, days),
        (year, mine, came, after),
        (SCALARS, INSIDE, INSIDE, ANYWHERE),
        [(rows, LANES), (days * BLOCK, LANES)],
        [],
        days * FULL * LANES,
        3 * 4 * days * FULL * LANES,
    )
    return send, keep, token


def cross_kernel(days, year_ref, mine_ref, keep_ref, came_ref, after_ref, send_ref, own_ref, token_ref):
    low_half = year_ref[0] < 2
    token_ref[...] = jnp.zeros_like(token_ref)
    _, lane = iotas((BLOCK, LANES))

    def day(i, carry):
        src = pl.multiple_of(i * CROSS, CROSS)
        own = pl.multiple_of(i * BLOCK, BLOCK)
        dst = pl.multiple_of(i * OWN, OWN)
        top = mine_ref[pl.ds(src, BLOCK)] + came_ref[pl.ds(src, BLOCK)]
        bottom = mine_ref[pl.ds(src + BLOCK, BLOCK)] + came_ref[pl.ds(src + BLOCK, BLOCK)]
        packed = keep_ref[pl.ds(own, BLOCK)] + came_ref[pl.ds(src + LANES, BLOCK)]
        first = jnp.where(lane < BLOCK, top, swap(bottom))
        second = jnp.where(lane < BLOCK, swap(top), bottom)
        send_ref[pl.ds(dst, BLOCK)] = packed
        own_ref[pl.ds(dst, BLOCK)] = packed
        send_ref[pl.ds(dst + BLOCK, BLOCK)] = jnp.where(low_half, top, second)
        own_ref[pl.ds(dst + BLOCK, BLOCK)] = jnp.where(low_half, bottom, first)
        return carry

    lax.fori_loop(0, days, day, 0)
    small = mine_ref[days * CROSS :] + came_ref[days * CROSS :]
    send_ref[days * OWN :] = small
    own_ref[days * OWN :] = small


def cross(year, mine, keep, came, days, after):
    rows = days * OWN + small_rows(days)
    (send, own), token = call(
        functools.partial(cross_kernel, days),
        (year, mine, keep, came, after),
        (SCALARS, INSIDE, INSIDE, INSIDE, ANYWHERE),
        [(rows, LANES)] * 2,
        [],
        days * CROSS * LANES,
        3 * 4 * days * CROSS * LANES,
    )
    return send, own, token


def is_outer(year):
    return (year == 0) | (year == 3)


def day_rows(year, number, i, mine_ref, own_ref, came_ref):
    outer, low_half = is_outer(year), year < 2
    row, lane = iotas((BLOCK, LANES))
    alone = jnp.where(own_side(row, lane, low_half), half_rows(mine_ref, i, low_half), 0.0)
    start = i * OWN
    top = jnp.where(outer, came_ref[start : start + BLOCK] + alone, own_ref[start : start + BLOCK])
    middle = start + BLOCK
    bottom = jnp.where(outer, came_ref[middle : middle + BLOCK], own_ref[middle : middle + BLOCK])
    at = number * OWN + SMALL * i
    small = jnp.where(outer, came_ref[at : at + SMALL], own_ref[at : at + SMALL])
    kept = mine_ref[number * FULL + SMALL * i : number * FULL + SMALL * i + 1]
    diagonal = small[:1] + jnp.where(outer & ~low_half & (lane[:1] < BLOCK), kept, 0.0)
    return jnp.concatenate([top, bottom], axis=0), diagonal, small[1:2], small[2:3]


def day_counts(year, number, own_ref, came_ref):
    at = number * OWN + SMALL * number
    return jnp.where(is_outer(year), came_ref[at : at + 1], own_ref[at : at + 1])


def pick_kernel(runs, year_ref, mine_ref, own_ref, came_ref, after_ref, *refs):
    outs, token_ref = refs[:-1], refs[-1]
    year = year_ref[0]
    token_ref[...] = jnp.zeros_like(token_ref)
    days = length(runs)
    counts = day_counts(year, days, own_ref, came_ref)
    at = 0
    for (_, number), out_ref in zip(runs, outs):
        small = number * OWN
        for i in range(number):
            rows, *lines = day_rows(year, days, at + i, mine_ref, own_ref, came_ref)
            out_ref[i * OWN : (i + 1) * OWN] = rows
            for k, line in enumerate(lines):
                out_ref[small + SMALL * i + k : small + SMALL * i + k + 1] = line
        last = small + SMALL * number
        out_ref[last : last + 1] = pltpu.roll(counts, (LANES - at) % LANES, 1)
        at += number


def pick(year, mine, own, came, runs, after):
    return call(
        functools.partial(pick_kernel, runs),
        (year, mine, own, came, after),
        (SCALARS, INSIDE, INSIDE, INSIDE, ANYWHERE),
        [(size * OWN + small_rows(size), LANES) for _, size in runs],
        [],
        0,
        2 * 4 * own.size,
    )


def unpack(year, rows, diagonal):
    odd = lax.rem(year, 2) == 1
    low_half = year < 2
    row, lane = iotas((BLOCK, LANES))
    turned = rows.T
    top, bottom = rows[:BLOCK], rows[BLOCK:]
    top_turned, bottom_turned = turned[:BLOCK], turned[BLOCK:]
    upper = jnp.where(lane < BLOCK, jnp.where(row <= lane, top, top_turned), top)
    lower = swap(jnp.where(row > lane, top, top_turned))
    diagonal = jnp.where(low_half, diagonal, swap(diagonal))
    lower = jnp.where(row == lane - BLOCK, diagonal, lower)
    lower = jnp.where(lane < BLOCK, bottom_turned, lower)
    packed = jnp.where(odd, lower, upper)
    across = jnp.where(lane < BLOCK, swap(top_turned), bottom_turned)
    return jnp.where(low_half, packed, across), jnp.where(low_half, bottom, packed)


def windows_kernel(places, days, year_ref, *refs):
    parts = refs[: len(places)]
    win_ref, small_ref, token_ref, packed_ref = refs[len(places) + 1 :]
    token_ref[...] = jnp.zeros_like(token_ref)
    year = year_ref[0]
    extended = days + 2 * HALF
    where = {}
    for (place, number), ref in zip(places, parts):
        for i in range(number):
            where[place + i] = (ref, i, number * OWN)

    def sums(load, store):
        def add(a, b):
            return b if a is None else a if b is None else a + b

        def level(table, hop):
            return [add(table[k], table[k + hop]) for k in range(len(table) - hop)]

        ones = [load(*where[k]) if k in where else None for k in range(extended)]
        twos = level(ones, 1)
        fours = level(twos, 2)
        eights = level(fours, 4)
        for d in range(days):
            store(d, add(add(eights[d], fours[d + 8]), add(twos[d + 12], ones[d + 14])))

    def strip(s, carry):
        at = pl.multiple_of(s * SUBLANES, SUBLANES)

        def store(d, value):
            packed_ref[d, pl.ds(at, SUBLANES)] = value

        sums(lambda ref, i, small: ref[pl.ds(i * OWN + at, SUBLANES)], store)
        return carry

    lax.fori_loop(0, OWN // SUBLANES, strip, 0)

    for row in range(SMALL):

        def store_row(d, value):
            small_ref[row, d : d + 1] = value

        sums(lambda ref, i, small: ref[small + SMALL * i + row : small + SMALL * i + row + 1], store_row)

    lane = lax.broadcasted_iota(jnp.int32, (1, LANES), 1)

    def load_count(ref, i, small):
        last = small + SMALL * (small // OWN)
        count = jnp.sum(jnp.where(lane == i, ref[last : last + 1], 0.0), axis=1, keepdims=True)
        return jnp.broadcast_to(count, (1, LANES))

    def store_count(d, value):
        small_ref[SMALL, d : d + 1] = value

    sums(load_count, store_count)

    def day(d, carry):
        left, right = unpack(year, packed_ref[d], small_ref[0, pl.ds(d, 1)])
        win_ref[d, :, :LANES] = left
        win_ref[d, :, LANES:] = right
        return carry

    lax.fori_loop(0, days, day, 0, unroll=True)


def windows(year, parts, places, days, after):
    (win, small), token = call(
        functools.partial(windows_kernel, places, days),
        (year, *parts, after),
        [SCALARS] + [INSIDE] * len(parts) + [ANYWHERE],
        [(days, BLOCK, 2 * LANES), (SMALL + 1, days, LANES)],
        [pltpu.VMEM((days, OWN, LANES), jnp.float32)],
        6 * days * BLOCK * 2 * LANES,
        8 * days * BLOCK * 2 * LANES,
    )
    return win, small, token


def finish_kernel(places, pieces, year_ref, win_ref, small_ref, *refs):
    held, (after_ref, cov_ref, mean_ref, token_ref, formed, sent) = refs[: 3 * len(places)], refs[3 * len(places) :]
    token_ref[...] = jnp.zeros_like(token_ref)
    year = year_ref[0]
    days = win_ref.shape[0]
    lane = lax.broadcasted_iota(jnp.int32, (1, LANES), 1)
    day_of = lax.broadcasted_iota(jnp.int32, (days, LANES), 0)
    low, high, count = small_ref[1], small_ref[2], small_ref[SMALL]
    extras = []
    for p, (place, number) in enumerate(places):
        arrays = held[3 * p : 3 * p + 3]
        numbers = day_counts(year, number, *arrays[1:])
        for i in range(number):
            rows, diagonal, more_low, more_high = day_rows(year, number, i, *arrays)
            inside = jnp.abs(day_of - (place + i)) <= HALF
            low += jnp.where(inside, more_low, 0.0)
            high += jnp.where(inside, more_high, 0.0)
            extra = jnp.sum(jnp.where(lane == i, numbers, 0.0), axis=1, keepdims=True)
            count += jnp.where(inside, extra, 0.0)
            extras.append((place + i, unpack(year, rows, diagonal)))
    low = low / count
    high = high / count
    own = jnp.where(year < 2, low, high)
    own = jnp.where(lax.rem(year, 2) == 1, swap(own), own)
    mean_ref[:, 0] = own[:, :BLOCK]
    turned = jnp.concatenate([own, jnp.zeros((LANES - days, LANES), jnp.float32)], axis=0).T
    scale = 1.0 / (count - 1.0)
    low = low * (count * scale)
    high = high * (count * scale)
    copies = []
    for first, size in pieces:
        for d in range(first, first + size):
            left, right = win_ref[d, :, :LANES], win_ref[d, :, LANES:]
            for at, (more_left, more_right) in extras:
                if abs(d - at) <= HALF:
                    left, right = left + more_left, right + more_right
            column = turned[:BLOCK, d : d + 1]
            factor = scale[d : d + 1]
            formed[d, :, :LANES] = left * factor - column * low[d : d + 1]
            formed[d, :, LANES:] = right * factor - column * high[d : d + 1]
        piece = pl.ds(first, size)
        copy = pltpu.make_async_copy(formed.at[piece], cov_ref.at[0, piece], sent.at[len(copies)])
        copy.start()
        copies.append(copy)
    for copy in copies:
        copy.wait()


def finish(year, win, small, held, places, after):
    days, _, width = win.shape
    size = -(-days // 3)
    pieces = tuple((first, min(size, days - first)) for first in range(0, days, size))
    flat = [array for arrays in held for array in arrays]
    (covariance, mean), _ = call(
        functools.partial(finish_kernel, places, pieces),
        (year, win, small, *flat, after),
        [SCALARS] + [INSIDE] * (2 + len(flat)) + [ANYWHERE],
        [(1, days, BLOCK, width), (days, 1, BLOCK)],
        [pltpu.VMEM((days, BLOCK, width), jnp.float32), pltpu.SemaphoreType.DMA((len(pieces),))],
        6 * days * BLOCK * width,
        8 * days * BLOCK * width,
        outs=[ANYWHERE, INSIDE],
    )
    return covariance, mean


def plan(days):
    parts = [((0, 4),), ((days - 5, 5),), ((4, HALF - 4), (days - HALF, HALF - 5))]
    at, left = HALF, days - 2 * HALF
    for size in (left - 5, 3, 2):
        parts.append(((at, size),))
        at += size
    return parts


ORDER = (
    ("gram", 0),
    ("gram", 1),
    ("gram", 2, 3, 4, 5),
    ("inner", 0),
    ("inner", 1),
    ("cross", 0),
    ("inner", 2),
    ("pick", 0),
    ("cross", 1),
    ("inner", 3),
    ("pick", 1),
    ("cross", 2),
    ("inner", 4),
    ("cross", 3),
    ("inner", 5),
    ("pick", 2),
    ("cross", 4),
    ("pick", 3),
    ("cross", 5),
    ("windows",),
    ("finish", 4, 5),
)


def shards(samples, counts):
    days = samples.shape[0]
    day_size = lax.axis_size("day")
    position = lax.axis_index("year")
    year = position.astype(jnp.int32)[None]
    inward = [(0, 1), (3, 2)]
    between = [(1, 2), (2, 1)]
    outward = [(1, 0), (2, 3)]
    right = [(i, (i + 1) % day_size) for i in range(day_size)]
    left = [((i + 1) % day_size, i) for i in range(day_size)]
    counts = jnp.transpose(counts, (0, 2, 1))
    parts = plan(days)
    token = [jnp.zeros(TOKEN, jnp.float32)]
    mine, sums, rows = {}, {}, {}
    totals, places, halos = [], [], {}

    def gram_step(*ks):
        nonlocal token
        outs, token = gram(samples, counts, year, tuple(parts[k] for k in ks), token)
        for k, (out, sent) in zip(ks, outs):
            mine[k] = (out, lax.ppermute(sent, "year", inward))

    def inner_step(k):
        nonlocal token
        send, keep, token = inner(year, *mine[k], length(parts[k]), token)
        sums[k] = (send, keep, lax.ppermute(send, "year", between))

    def cross_step(k):
        nonlocal token
        send, own, token = cross(year, *sums[k], length(parts[k]), token)
        rows[k] = (mine[k][0], own, lax.ppermute(send, "year", outward))

    def pick_step(k):
        nonlocal token
        outs, token = pick(year, *rows[k], parts[k], token)
        for (start, size), out in zip(parts[k], outs):
            totals.append(out)
            places.append((start + HALF, size))
            if start < HALF:
                totals.append(lax.ppermute(out, "day", left))
                places.append((start + HALF + days, size))
                halos.setdefault(k, []).append(totals[-1])
            elif start >= days - HALF:
                totals.append(lax.ppermute(out, "day", right))
                places.append((start + HALF - days, size))
                halos.setdefault(k, []).append(totals[-1])

    def halo_step(k):
        nonlocal token
        token = [*token, *halos[k]]

    def windows_step():
        nonlocal token
        win, small, token = windows(year, totals, tuple(places), days, token)
        return win, small

    def finish_step(*ks):
        last = tuple(parts[k][0] for k in ks)
        return finish(year, *held, [rows[k] for k in ks], last, token)

    steps = {
        "gram": gram_step,
        "inner": inner_step,
        "cross": cross_step,
        "pick": pick_step,
        "halo": halo_step,
        "windows": windows_step,
        "finish": finish_step,
    }
    held = None
    for name, *ks in ORDER:
        result = steps[name](*ks)
        held = result if result else held
    covariance, mean = held
    return covariance, jnp.transpose(mean, (1, 0, 2))


def solution(mesh):
    placed = (P("day", "year", "region", None), P("region", "day", "year"))
    return jax.shard_map(
        shards,
        mesh=mesh,
        in_specs=placed,
        out_specs=(P("region", "day", "year", None), P("region", "day", "year")),
        check_vma=False,
    )
```

```python
import functools

import jax
import jax.numpy as jnp
from jax import lax
from jax.experimental import pallas as pl
from jax.experimental.pallas import tpu as pltpu
from jax.sharding import PartitionSpec as P

HALF = 7
LANES = 128
BLOCK = 64
SUBLANES = 8
FULL, CROSS, OWN = 4 * BLOCK, 3 * BLOCK, 2 * BLOCK
PAIR = BLOCK + BLOCK // 2
SMALL = 3
AHEAD = 3
TOKEN = (SUBLANES, LANES)
SCALARS = pl.BlockSpec(memory_space=pltpu.SMEM)
INSIDE = pl.BlockSpec(memory_space=pltpu.VMEM)
ANYWHERE = pl.BlockSpec(memory_space=pl.ANY)


def small_rows(days):
    return -(-(SMALL * days + 1) // SUBLANES) * SUBLANES


def length(runs):
    return sum(size for _, size in runs)


def call(kernel, args, specs, shapes, scratch, flops, moved, mebibytes=16, outs=None):
    results = pl.pallas_call(
        kernel,
        in_specs=list(specs),
        out_specs=(list(outs) if outs else [INSIDE] * len(shapes)) + [INSIDE],
        out_shape=[jax.ShapeDtypeStruct(shape, jnp.float32) for shape in list(shapes) + [TOKEN]],
        scratch_shapes=scratch,
        cost_estimate=pl.CostEstimate(flops=0, bytes_accessed=0, transcendentals=0),
        compiler_params=pltpu.CompilerParams(vmem_limit_bytes=mebibytes * 1024 * 1024),
    )(*args)
    return results[:-1], results[-1]


def sent_rows(days):
    return days * CROSS + days // 2 * PAIR + days % 2 * BLOCK


def iotas(shape):
    return lax.broadcasted_iota(jnp.int32, shape, 0), lax.broadcasted_iota(jnp.int32, shape, 1)


def swap(block):
    return pltpu.roll(block, BLOCK, 1)


def pack_quadrant(quadrant):
    top, bottom = quadrant[:BLOCK], swap(quadrant[BLOCK:])
    row, lane = iotas((BLOCK, LANES))
    packed = jnp.where((lane < BLOCK) & (row > lane), bottom, top)
    diagonal = jnp.sum(jnp.where(row == lane, bottom, 0.0), axis=0, keepdims=True)
    return packed, diagonal


def own_side(row, lane, low_half):
    ahead = jnp.where(low_half, lane - row, row - lane - 1)
    return (lane < BLOCK) & (ahead >= 0)


def half_rows(ref, i, low_half):
    return ref[pl.ds(pl.multiple_of(i * FULL + LANES + jnp.where(low_half, 0, BLOCK), BLOCK), BLOCK)]


def pack_sent(days, low_half, mine_ref, sent_ref):
    row, lane = iotas((BLOCK, LANES))
    own = own_side(row, lane, low_half)
    small, at = days * FULL, sent_rows(days)
    sent_ref[at:] = mine_ref[small:]

    def day(i, carry):
        src = pl.multiple_of(i * FULL, FULL)
        dst = pl.multiple_of(i * CROSS, CROSS)
        sent_ref[pl.ds(dst, LANES)] = mine_ref[pl.ds(src, LANES)]
        sent_ref[pl.ds(dst + LANES, BLOCK)] = half_rows(mine_ref, i, ~low_half)
        diagonal = jnp.sum(jnp.where(row == lane, half_rows(mine_ref, i, low_half), 0.0), axis=0, keepdims=True)
        kept = mine_ref[pl.ds(small + SMALL * i, 1)]
        sent_ref[pl.ds(at + SMALL * i, 1)] = jnp.where(low_half | (lane[:1] >= BLOCK), kept, diagonal)
        return carry

    lax.fori_loop(0, days, day, 0)

    def pair(p, carry):
        first, second = half_rows(mine_ref, 2 * p, low_half), half_rows(mine_ref, 2 * p + 1, low_half)
        turned = jnp.concatenate([first, second], axis=0).T[:BLOCK]
        below = jnp.where(low_half, first, turned)
        above = jnp.where(low_half, swap(turned), second)
        triangles = jnp.where(row > lane, below, above)
        dst = pl.multiple_of(days * CROSS + p * PAIR, PAIR // 3)
        sent_ref[pl.ds(dst, BLOCK)] = jnp.where(lane < BLOCK, swap(first), second)
        rest = jnp.where(lane[: BLOCK // 2] < BLOCK, triangles[: BLOCK // 2], swap(triangles[BLOCK // 2 :]))
        sent_ref[pl.ds(dst + BLOCK, BLOCK // 2)] = rest
        return carry

    lax.fori_loop(0, days // 2, pair, 0)
    if days % 2:
        last = days * CROSS + days // 2 * PAIR
        sent_ref[last : last + BLOCK] = jnp.where(own, 0.0, half_rows(mine_ref, days - 1, low_half))


def gram_kernel(parts, counts_ref, year_ref, samples_ref, after_ref, *refs):
    outs, sents = refs[: len(parts)], refs[len(parts) : 2 * len(parts)]
    token_ref, held, arrived = refs[2 * len(parts) :]
    low_half = year_ref[0] < 2
    groups, slots, width = held.shape[1:]
    lane = lax.broadcasted_iota(jnp.int32, (1, LANES), 1)
    rank = lax.broadcasted_iota(jnp.int32, (1, slots), 1)
    token_ref[...] = jnp.zeros_like(token_ref)

    def copies(day, slot):
        return [
            pltpu.make_async_copy(samples_ref.at[day, g], held.at[slot, g], arrived.at[slot, g])
            for g in range(groups)
        ]

    order = [start + i for runs in parts for start, number in runs for i in range(number)]
    for slot in range(min(AHEAD, len(order))):
        for copy in copies(order[slot], slot):
            copy.start()

    def later(slot):
        day, at = jnp.int32(0), 0
        for runs in parts:
            for start, number in runs:
                inside = (slot + AHEAD >= at) & (slot + AHEAD < at + number)
                day = jnp.where(inside, start + slot + AHEAD - at, day)
                at += number

        @pl.when(slot + AHEAD < len(order))
        def _():
            for copy in copies(day, slot + AHEAD):
                copy.start()

    slot = 0
    for runs, out_ref, sent_ref in zip(parts, outs, sents):
        days = length(runs)
        small = days * FULL
        out_ref[small:] = jnp.zeros((small_rows(days), LANES), jnp.float32)
        numbers = jnp.zeros((1, LANES), jnp.int32)
        at = 0
        for start, number in runs:

            def day(i, numbers, start=start, at=at, slot=slot, out_ref=out_ref, small=small):
                gram = jnp.zeros((width, width), jnp.float32)
                total = jnp.zeros((1, width), jnp.float32)
                later(slot + i)
                for copy in copies(start + i, slot + i):
                    copy.wait()
                for g in range(groups):
                    count = counts_ref[0, g, start + i]
                    numbers += jnp.where(lane == at + i, count, 0)
                    block = held[slot + i, g]
                    left = jnp.concatenate([block.T, jnp.ones((2 * SUBLANES, slots), block.dtype)], axis=0)
                    left = jnp.where(rank < count, left, jnp.zeros_like(left))
                    product = jnp.dot(left, block, preferred_element_type=jnp.float32)
                    gram += product[:width]
                    total += product[width : width + 1]
                base = pl.multiple_of((at + i) * FULL, FULL)
                low, diagonal_low = pack_quadrant(gram[:LANES, :LANES])
                high, diagonal_high = pack_quadrant(gram[LANES:, LANES:])
                out_ref[pl.ds(base, LANES)] = gram[:LANES, LANES:]
                out_ref[pl.ds(base + LANES, BLOCK)] = low
                out_ref[pl.ds(base + LANES + BLOCK, BLOCK)] = high
                row = small + SMALL * (at + i)
                out_ref[pl.ds(row, 1)] = diagonal_high + swap(diagonal_low)
                out_ref[pl.ds(row + 1, 1)] = total[:, :LANES]
                out_ref[pl.ds(row + 2, 1)] = total[:, LANES:]
                return numbers

            numbers = lax.fori_loop(0, number, day, numbers)
            at += number
            slot += number
        last = small + SMALL * days
        out_ref[last : last + 1] = numbers.astype(jnp.float32)
        pack_sent(days, low_half, out_ref, sent_ref)


def gram(samples, counts, year, parts, after):
    _, groups, slots, width = samples.shape
    days = sum(length(runs) for runs in parts)
    rows = [length(runs) * FULL + small_rows(length(runs)) for runs in parts]
    rows += [sent_rows(length(runs)) + small_rows(length(runs)) for runs in parts]
    outs, token = call(
        functools.partial(gram_kernel, parts),
        (counts, year, samples, after),
        (SCALARS, SCALARS, ANYWHERE, ANYWHERE),
        [(size, LANES) for size in rows],
        [
            pltpu.VMEM((days, groups, slots, width), samples.dtype),
            pltpu.SemaphoreType.DMA((days, groups)),
        ],
        2 * days * groups * slots * width * width,
        2 * days * groups * slots * width + 4 * sum(rows) * LANES,
        44,
    )
    return list(zip(outs[: len(parts)], outs[len(parts) :])), token


def inner_kernel(days, year_ref, mine_ref, came_ref, after_ref, send_ref, keep_ref, token_ref):
    low_half = year_ref[0] < 2
    token_ref[...] = jnp.zeros_like(token_ref)
    row, lane = iotas((BLOCK, LANES))
    at = sent_rows(days)

    def day(i, carry):
        src = pl.multiple_of(i * FULL, FULL)
        dst = pl.multiple_of(i * CROSS, CROSS)
        send_ref[pl.ds(dst, LANES)] = mine_ref[pl.ds(src, LANES)] + came_ref[pl.ds(dst, LANES)]
        other = pl.ds(dst + LANES, BLOCK)
        send_ref[other] = half_rows(mine_ref, i, ~low_half) + came_ref[other]
        return carry

    lax.fori_loop(0, days, day, 0)

    def pair(p, carry):
        src = pl.multiple_of(days * CROSS + p * PAIR, PAIR // 3)
        blocks = came_ref[pl.ds(src, BLOCK)]
        rest = came_ref[pl.ds(src + BLOCK, BLOCK // 2)]
        triangles = jnp.concatenate([rest, swap(rest)], axis=0)
        turned = jnp.concatenate([triangles, jnp.zeros_like(triangles)], axis=0).T[:BLOCK]
        side = jnp.where(low_half, row - lane, lane - row)
        for k, block in enumerate((swap(blocks), blocks)):
            i = 2 * p + k
            triangle = jnp.where(low_half, (triangles, turned)[k], (turned, triangles)[k])
            diagonal = jnp.where(low_half, 0.0, came_ref[pl.ds(at + SMALL * i, 1)])
            triangle = jnp.where(side > 0, triangle, jnp.where(side == 0, diagonal, 0.0))
            keep_ref[pl.ds(pl.multiple_of(i * BLOCK, BLOCK), BLOCK)] = half_rows(mine_ref, i, low_half) + jnp.where(
                lane < BLOCK, triangle, block
            )
        return carry

    lax.fori_loop(0, days // 2, pair, 0)
    if days % 2:
        last = at - BLOCK
        keep_ref[(days - 1) * BLOCK :] = half_rows(mine_ref, days - 1, low_half) + came_ref[last:at]
    row, lane = iotas((small_rows(days), LANES))
    diagonals = (lax.rem(row, SMALL) == 0) & (row < SMALL * days) & (lane < BLOCK)
    came = jnp.where(diagonals & ~low_half, 0.0, came_ref[at:])
    send_ref[days * CROSS :] = mine_ref[days * FULL :] + came


def inner(year, mine, came, days, after):
    rows = days * CROSS + small_rows(days)
    (send, keep), token = call(
        functools.partial(inner_kernel, days),
        (year, mine, came, after),
        (SCALARS, INSIDE, INSIDE, ANYWHERE),
        [(rows, LANES), (days * BLOCK, LANES)],
        [],
        days * FULL * LANES,
        3 * 4 * days * FULL * LANES,
    )
    return send, keep, token


def own_size(days):
    return days * OWN + small_rows(days)


def cross_kernel(sizes, year_ref, *refs):
    held, (_, send_ref, *owns, token_ref) = refs[: 3 * len(sizes)], refs[3 * len(sizes) :]
    low_half = year_ref[0] < 2
    token_ref[...] = jnp.zeros_like(token_ref)
    _, lane = iotas((BLOCK, LANES))
    base = 0
    for p, (days, own_ref) in enumerate(zip(sizes, owns)):
        mine_ref, keep_ref, came_ref = held[3 * p : 3 * p + 3]

        def day(i, carry, mine_ref=mine_ref, keep_ref=keep_ref, came_ref=came_ref, own_ref=own_ref, base=base):
            src = pl.multiple_of(i * CROSS, CROSS)
            own = pl.multiple_of(i * BLOCK, BLOCK)
            dst = pl.multiple_of(i * OWN, OWN)
            out = pl.multiple_of(base + i * OWN, SUBLANES)
            top = mine_ref[pl.ds(src, BLOCK)] + came_ref[pl.ds(src, BLOCK)]
            bottom = mine_ref[pl.ds(src + BLOCK, BLOCK)] + came_ref[pl.ds(src + BLOCK, BLOCK)]
            packed = keep_ref[pl.ds(own, BLOCK)] + came_ref[pl.ds(src + LANES, BLOCK)]
            first = jnp.where(lane < BLOCK, top, swap(bottom))
            second = jnp.where(lane < BLOCK, swap(top), bottom)
            send_ref[pl.ds(out, BLOCK)] = packed
            own_ref[pl.ds(dst, BLOCK)] = packed
            send_ref[pl.ds(out + BLOCK, BLOCK)] = jnp.where(low_half, top, second)
            own_ref[pl.ds(dst + BLOCK, BLOCK)] = jnp.where(low_half, bottom, first)
            return carry

        lax.fori_loop(0, days, day, 0)
        small = mine_ref[days * CROSS :] + came_ref[days * CROSS :]
        send_ref[base + days * OWN : base + own_size(days)] = small
        own_ref[days * OWN :] = small
        base += own_size(days)


def cross(year, held, sizes, after):
    rows = [own_size(days) for days in sizes]
    (send, *owns), token = call(
        functools.partial(cross_kernel, sizes),
        (year, *(array for arrays in held for array in arrays), after),
        [SCALARS] + [INSIDE] * (3 * len(sizes)) + [ANYWHERE],
        [(sum(rows), LANES)] + [(size, LANES) for size in rows],
        [],
        sum(sizes) * CROSS * LANES,
        3 * 4 * sum(sizes) * CROSS * LANES,
    )
    return send, owns, token


def is_outer(year):
    return (year == 0) | (year == 3)


def day_rows(year, number, i, mine_ref, own_ref, came_ref):
    outer, low_half = is_outer(year), year < 2
    row, lane = iotas((BLOCK, LANES))
    alone = jnp.where(own_side(row, lane, low_half), half_rows(mine_ref, i, low_half), 0.0)
    start = i * OWN
    top = jnp.where(outer, came_ref[start : start + BLOCK] + alone, own_ref[start : start + BLOCK])
    middle = start + BLOCK
    bottom = jnp.where(outer, came_ref[middle : middle + BLOCK], own_ref[middle : middle + BLOCK])
    at = number * OWN + SMALL * i
    small = jnp.where(outer, came_ref[at : at + SMALL], own_ref[at : at + SMALL])
    kept = mine_ref[number * FULL + SMALL * i : number * FULL + SMALL * i + 1]
    diagonal = small[:1] + jnp.where(outer & ~low_half & (lane[:1] < BLOCK), kept, 0.0)
    return jnp.concatenate([top, bottom], axis=0), diagonal, small[1:2], small[2:3]


def day_counts(year, number, own_ref, came_ref):
    at = number * OWN + SMALL * number
    return jnp.where(is_outer(year), came_ref[at : at + 1], own_ref[at : at + 1])


def views(refs, bases, sizes):
    held = []
    for p, (base, size) in enumerate(zip(bases, sizes)):
        mine_ref, own_ref, came_ref = refs[3 * p : 3 * p + 3]
        held.append((mine_ref, own_ref, came_ref.at[pl.ds(base, own_size(size))]))
    return held


def pick_kernel(bases, sizes, moves, year_ref, *refs):
    held = views(refs, bases, sizes)
    (_, *outs, token_ref) = refs[3 * len(sizes) :]
    year = year_ref[0]
    token_ref[...] = jnp.zeros_like(token_ref)
    lane = lax.broadcasted_iota(jnp.int32, (1, LANES), 1)
    counts = [day_counts(year, size, *arrays[1:]) for size, arrays in zip(sizes, held)]
    for stretch, out_ref in zip(moves, outs):
        small = len(stretch) * OWN
        numbers = jnp.zeros((1, LANES), jnp.float32)
        for k, (p, i) in enumerate(stretch):
            rows, *lines = day_rows(year, sizes[p], i, *held[p])
            out_ref[k * OWN : (k + 1) * OWN] = rows
            for l, line in enumerate(lines):
                at = small + SMALL * k + l
                out_ref[at : at + 1] = line
            number = jnp.sum(jnp.where(lane == i, counts[p], 0.0), axis=1, keepdims=True)
            numbers += jnp.where(lane == k, number, 0.0)
        last = small + SMALL * len(stretch)
        out_ref[last : last + 1] = numbers


def pick(year, held, bases, sizes, moves, after):
    return call(
        functools.partial(pick_kernel, bases, sizes, moves),
        (year, *(array for arrays in held for array in arrays), after),
        [SCALARS] + [INSIDE] * (3 * len(sizes)) + [ANYWHERE],
        [(own_size(len(stretch)), LANES) for stretch in moves],
        [],
        0,
        2 * 4 * sum(sizes) * OWN * LANES,
    )


def unpack(year, rows, diagonal):
    odd = lax.rem(year, 2) == 1
    low_half = year < 2
    row, lane = iotas((BLOCK, LANES))
    turned = rows.T
    top, bottom = rows[:BLOCK], rows[BLOCK:]
    top_turned, bottom_turned = turned[:BLOCK], turned[BLOCK:]
    upper = jnp.where(lane < BLOCK, jnp.where(row <= lane, top, top_turned), top)
    lower = swap(jnp.where(row > lane, top, top_turned))
    diagonal = jnp.where(low_half, diagonal, swap(diagonal))
    lower = jnp.where(row == lane - BLOCK, diagonal, lower)
    lower = jnp.where(lane < BLOCK, bottom_turned, lower)
    packed = jnp.where(odd, lower, upper)
    across = jnp.where(lane < BLOCK, swap(top_turned), bottom_turned)
    return jnp.where(low_half, packed, across), jnp.where(low_half, bottom, packed)


def windows_kernel(places, days, year_ref, *refs):
    parts = refs[: len(places)]
    win_ref, small_ref, token_ref, packed_ref = refs[len(places) + 1 :]
    token_ref[...] = jnp.zeros_like(token_ref)
    year = year_ref[0]
    extended = days + 2 * HALF
    where = {}
    for (place, number), ref in zip(places, parts):
        for i in range(number):
            where[place + i] = (ref, i, number * OWN)

    def sums(load, store):
        def add(a, b):
            return b if a is None else a if b is None else a + b

        def level(table, hop):
            return [add(table[k], table[k + hop]) for k in range(len(table) - hop)]

        ones = [load(*where[k]) if k in where else None for k in range(extended)]
        twos = level(ones, 1)
        fours = level(twos, 2)
        eights = level(fours, 4)
        for d in range(days):
            store(d, add(add(eights[d], fours[d + 8]), add(twos[d + 12], ones[d + 14])))

    def strip(s, carry):
        at = pl.multiple_of(s * SUBLANES, SUBLANES)

        def store(d, value):
            packed_ref[d, pl.ds(at, SUBLANES)] = value

        sums(lambda ref, i, small: ref[pl.ds(i * OWN + at, SUBLANES)], store)
        return carry

    lax.fori_loop(0, OWN // SUBLANES, strip, 0)

    for row in range(SMALL):

        def store_row(d, value):
            small_ref[row, d : d + 1] = value

        sums(lambda ref, i, small: ref[small + SMALL * i + row : small + SMALL * i + row + 1], store_row)

    lane = lax.broadcasted_iota(jnp.int32, (1, LANES), 1)

    def load_count(ref, i, small):
        last = small + SMALL * (small // OWN)
        count = jnp.sum(jnp.where(lane == i, ref[last : last + 1], 0.0), axis=1, keepdims=True)
        return jnp.broadcast_to(count, (1, LANES))

    def store_count(d, value):
        small_ref[SMALL, d : d + 1] = value

    sums(load_count, store_count)

    def day(d, carry):
        left, right = unpack(year, packed_ref[d], small_ref[0, pl.ds(d, 1)])
        win_ref[d, :, :LANES] = left
        win_ref[d, :, LANES:] = right
        return carry

    lax.fori_loop(0, days, day, 0, unroll=True)


def windows(year, parts, places, days, after):
    (win, small), token = call(
        functools.partial(windows_kernel, places, days),
        (year, *parts, after),
        [SCALARS] + [INSIDE] * len(parts) + [ANYWHERE],
        [(days, BLOCK, 2 * LANES), (SMALL + 1, days, LANES)],
        [pltpu.VMEM((days, OWN, LANES), jnp.float32)],
        6 * days * BLOCK * 2 * LANES,
        8 * days * BLOCK * 2 * LANES,
    )
    return win, small, token


def finish_kernel(bases, places, pieces, year_ref, win_ref, small_ref, *refs):
    held = views(refs, bases, [number for _, number in places])
    after_ref, cov_ref, mean_ref, token_ref, formed, sent = refs[3 * len(places) :]
    token_ref[...] = jnp.zeros_like(token_ref)
    year = year_ref[0]
    days = win_ref.shape[0]
    lane = lax.broadcasted_iota(jnp.int32, (1, LANES), 1)
    day_of = lax.broadcasted_iota(jnp.int32, (days, LANES), 0)
    low, high, count = small_ref[1], small_ref[2], small_ref[SMALL]
    extras = []
    for p, (place, number) in enumerate(places):
        arrays = held[p]
        numbers = day_counts(year, number, *arrays[1:])
        for i in range(number):
            rows, diagonal, more_low, more_high = day_rows(year, number, i, *arrays)
            inside = jnp.abs(day_of - (place + i)) <= HALF
            low += jnp.where(inside, more_low, 0.0)
            high += jnp.where(inside, more_high, 0.0)
            extra = jnp.sum(jnp.where(lane == i, numbers, 0.0), axis=1, keepdims=True)
            count += jnp.where(inside, extra, 0.0)
            extras.append((place + i, unpack(year, rows, diagonal)))
    low = low / count
    high = high / count
    own = jnp.where(year < 2, low, high)
    own = jnp.where(lax.rem(year, 2) == 1, swap(own), own)
    mean_ref[:, 0] = own[:, :BLOCK]
    turned = jnp.concatenate([own, jnp.zeros((LANES - days, LANES), jnp.float32)], axis=0).T
    scale = 1.0 / (count - 1.0)
    low = low * (count * scale)
    high = high * (count * scale)
    copies = []
    for first, size in pieces:
        for d in range(first, first + size):
            left, right = win_ref[d, :, :LANES], win_ref[d, :, LANES:]
            for at, (more_left, more_right) in extras:
                if abs(d - at) <= HALF:
                    left, right = left + more_left, right + more_right
            column = turned[:BLOCK, d : d + 1]
            factor = scale[d : d + 1]
            formed[d, :, :LANES] = left * factor - column * low[d : d + 1]
            formed[d, :, LANES:] = right * factor - column * high[d : d + 1]
        piece = pl.ds(first, size)
        copy = pltpu.make_async_copy(formed.at[piece], cov_ref.at[0, piece], sent.at[len(copies)])
        copy.start()
        copies.append(copy)
    for copy in copies:
        copy.wait()


def finish(year, win, small, held, bases, places, after):
    days, _, width = win.shape
    size = -(-days // 6)
    pieces = tuple((first, min(size, days - first)) for first in range(0, days, size))
    flat = [array for arrays in held for array in arrays]
    (covariance, mean), _ = call(
        functools.partial(finish_kernel, bases, places, pieces),
        (year, win, small, *flat, after),
        [SCALARS] + [INSIDE] * (2 + len(flat)) + [ANYWHERE],
        [(1, days, BLOCK, width), (days, 1, BLOCK)],
        [pltpu.VMEM((days, BLOCK, width), jnp.float32), pltpu.SemaphoreType.DMA((len(pieces),))],
        6 * days * BLOCK * width,
        8 * days * BLOCK * width,
        outs=[ANYWHERE, INSIDE],
    )
    return covariance, mean


def plan(days):
    parts = [((0, 4),), ((days - 5, 5),), ((4, HALF - 4), (days - HALF, HALF - 5))]
    at, left = HALF, days - 2 * HALF
    for size in (left - 5, 3, 2):
        parts.append(((at, size),))
        at += size
    return parts


ORDER = (
    ("gram", 0),
    ("gram", 1),
    ("gram", 2),
    ("inner", 0),
    ("gram", 3, 4, 5),
    ("inner", 1),
    ("cross", 0),
    ("inner", 2),
    ("pick", 0),
    ("cross", 1),
    ("inner", 3),
    ("pick", 1),
    ("cross", 2),
    ("inner", 4),
    ("cross", 3),
    ("pick", 2),
    ("inner", 5),
    ("cross", 4),
    ("cross", 5),
    ("pick", 3),
    ("windows",),
    ("finish", 4, 5),
)


def shards(samples, counts):
    days = samples.shape[0]
    day_size = lax.axis_size("day")
    position = lax.axis_index("year")
    year = position.astype(jnp.int32)[None]
    inward = [(0, 1), (3, 2)]
    between = [(1, 2), (2, 1)]
    outward = [(1, 0), (2, 3)]
    right = [(i, (i + 1) % day_size) for i in range(day_size)]
    left = [((i + 1) % day_size, i) for i in range(day_size)]
    counts = jnp.transpose(counts, (0, 2, 1))
    parts = plan(days)
    token = jnp.zeros(TOKEN, jnp.float32)
    mine, sums, rows = {}, {}, {}
    totals, places, bases = [], [], {}

    def gram_step(*ks):
        nonlocal token
        outs, token = gram(samples, counts, year, tuple(parts[k] for k in ks), token)
        for k, (out, sent) in zip(ks, outs):
            mine[k] = (out, lax.ppermute(sent, "year", inward))

    def inner_step(k):
        nonlocal token
        send, keep, token = inner(year, *mine[k], length(parts[k]), token)
        sums[k] = (send, keep, lax.ppermute(send, "year", between))

    def cross_step(*ks):
        nonlocal token
        sizes = [length(parts[k]) for k in ks]
        send, owns, token = cross(year, [sums[k] for k in ks], sizes, token)
        came = lax.ppermute(send, "year", outward)
        base = 0
        for k, own, size in zip(ks, owns, sizes):
            rows[k] = (mine[k][0], own, came)
            bases[k] = base
            base += own_size(size)

    def pick_step(*ks):
        nonlocal token
        found = {}
        for p, k in enumerate(ks):
            at = 0
            for start, size in parts[k]:
                found.update({start + i: (p, at + i) for i in range(size)})
                at += size
        low = [day for day in sorted(found) if day < HALF]
        high = [day for day in sorted(found) if day >= days - HALF]
        inside = [day for day in sorted(found) if HALF <= day < days - HALF]
        stretches = [stretch for stretch in (low, high, inside) if stretch]
        moves = [[found[day] for day in stretch] for stretch in stretches]
        sizes = [length(parts[k]) for k in ks]
        outs, token = pick(year, [rows[k] for k in ks], [bases[k] for k in ks], sizes, moves, token)
        for stretch, out in zip(stretches, outs):
            start, size = stretch[0], len(stretch)
            totals.append(out)
            places.append((start + HALF, size))
            if start < HALF:
                totals.append(lax.ppermute(out, "day", left))
                places.append((start + HALF + days, size))
            elif start >= days - HALF:
                totals.append(lax.ppermute(out, "day", right))
                places.append((start + HALF - days, size))

    def windows_step():
        nonlocal token
        win, small, token = windows(year, totals, tuple(places), days, token)
        return win, small

    def finish_step(*ks):
        last = tuple(parts[k][0] for k in ks)
        return finish(year, *held, [rows[k] for k in ks], [bases[k] for k in ks], last, token)

    steps = {
        "gram": gram_step,
        "inner": inner_step,
        "cross": cross_step,
        "pick": pick_step,
        "windows": windows_step,
        "finish": finish_step,
    }
    held = None
    for name, *ks in ORDER:
        result = steps[name](*ks)
        held = result if result else held
    covariance, mean = held
    return covariance, jnp.transpose(mean, (1, 0, 2))


def solution(mesh):
    placed = (P("day", "year", "region", None), P("region", "day", "year"))
    return jax.shard_map(
        shards,
        mesh=mesh,
        in_specs=placed,
        out_specs=(P("region", "day", "year", None), P("region", "day", "year")),
        check_vma=False,
    )
```

```python
import functools

import jax
import jax.numpy as jnp
from jax import lax
from jax.experimental import pallas as pl
from jax.experimental.pallas import tpu as pltpu
from jax.sharding import PartitionSpec as P

HALF = 7
LANES = 128
BLOCK = 64
SUBLANES = 8
FULL, CROSS, OWN = 4 * BLOCK, 3 * BLOCK, 2 * BLOCK
PAIR = BLOCK + BLOCK // 2
SMALL = 3
AHEAD = 3
TOKEN = (SUBLANES, LANES)
SCALARS = pl.BlockSpec(memory_space=pltpu.SMEM)
INSIDE = pl.BlockSpec(memory_space=pltpu.VMEM)
ANYWHERE = pl.BlockSpec(memory_space=pl.ANY)


def small_rows(days):
    return -(-(SMALL * days + 1) // SUBLANES) * SUBLANES


def length(runs):
    return sum(size for _, size in runs)


def call(kernel, args, specs, shapes, scratch, flops, moved, mebibytes=16, outs=None):
    results = pl.pallas_call(
        kernel,
        in_specs=list(specs),
        out_specs=(list(outs) if outs else [INSIDE] * len(shapes)) + [INSIDE],
        out_shape=[jax.ShapeDtypeStruct(shape, jnp.float32) for shape in list(shapes) + [TOKEN]],
        scratch_shapes=scratch,
        cost_estimate=pl.CostEstimate(flops=0, bytes_accessed=0, transcendentals=0),
        compiler_params=pltpu.CompilerParams(vmem_limit_bytes=mebibytes * 1024 * 1024),
    )(*args)
    return results[:-1], results[-1]


def sent_rows(days):
    return days * CROSS + days // 2 * PAIR + days % 2 * BLOCK


def iotas(shape):
    return lax.broadcasted_iota(jnp.int32, shape, 0), lax.broadcasted_iota(jnp.int32, shape, 1)


def swap(block):
    return pltpu.roll(block, BLOCK, 1)


def pack_quadrant(quadrant):
    top, bottom = quadrant[:BLOCK], swap(quadrant[BLOCK:])
    row, lane = iotas((BLOCK, LANES))
    packed = jnp.where((lane < BLOCK) & (row > lane), bottom, top)
    diagonal = jnp.sum(jnp.where(row == lane, bottom, 0.0), axis=0, keepdims=True)
    return packed, diagonal


def own_side(row, lane, low_half):
    ahead = jnp.where(low_half, lane - row, row - lane - 1)
    return (lane < BLOCK) & (ahead >= 0)


def half_rows(ref, i, low_half):
    return ref[pl.ds(pl.multiple_of(i * FULL + LANES + jnp.where(low_half, 0, BLOCK), BLOCK), BLOCK)]


def pack_sent(days, low_half, mine_ref, sent_ref):
    row, lane = iotas((BLOCK, LANES))
    own = own_side(row, lane, low_half)
    small, at = days * FULL, sent_rows(days)
    sent_ref[at:] = mine_ref[small:]

    def day(i, carry):
        src = pl.multiple_of(i * FULL, FULL)
        dst = pl.multiple_of(i * CROSS, CROSS)
        sent_ref[pl.ds(dst, LANES)] = mine_ref[pl.ds(src, LANES)]
        sent_ref[pl.ds(dst + LANES, BLOCK)] = half_rows(mine_ref, i, ~low_half)
        diagonal = jnp.sum(jnp.where(row == lane, half_rows(mine_ref, i, low_half), 0.0), axis=0, keepdims=True)
        kept = mine_ref[pl.ds(small + SMALL * i, 1)]
        sent_ref[pl.ds(at + SMALL * i, 1)] = jnp.where(low_half | (lane[:1] >= BLOCK), kept, diagonal)
        return carry

    lax.fori_loop(0, days, day, 0)

    def pair(p, carry):
        first, second = half_rows(mine_ref, 2 * p, low_half), half_rows(mine_ref, 2 * p + 1, low_half)
        turned = jnp.concatenate([first, second], axis=0).T[:BLOCK]
        below = jnp.where(low_half, first, turned)
        above = jnp.where(low_half, swap(turned), second)
        triangles = jnp.where(row > lane, below, above)
        dst = pl.multiple_of(days * CROSS + p * PAIR, PAIR // 3)
        sent_ref[pl.ds(dst, BLOCK)] = jnp.where(lane < BLOCK, swap(first), second)
        rest = jnp.where(lane[: BLOCK // 2] < BLOCK, triangles[: BLOCK // 2], swap(triangles[BLOCK // 2 :]))
        sent_ref[pl.ds(dst + BLOCK, BLOCK // 2)] = rest
        return carry

    lax.fori_loop(0, days // 2, pair, 0)
    if days % 2:
        last = days * CROSS + days // 2 * PAIR
        sent_ref[last : last + BLOCK] = jnp.where(own, 0.0, half_rows(mine_ref, days - 1, low_half))


def gram_kernel(parts, counts_from, year_ref, samples_ref, after_ref, *refs):
    outs, sents = refs[: len(parts)], refs[len(parts) : 2 * len(parts)]
    token_ref, held, arrived, counts_ref, counted = refs[2 * len(parts) :]
    low_half = year_ref[0] < 2
    groups, slots, width = held.shape[1:]
    lane = lax.broadcasted_iota(jnp.int32, (1, LANES), 1)
    rank = lax.broadcasted_iota(jnp.int32, (1, slots), 1)
    token_ref[...] = jnp.zeros_like(token_ref)

    def copies(day, slot):
        return [
            pltpu.make_async_copy(samples_ref.at[day, g], held.at[slot, g], arrived.at[slot, g])
            for g in range(groups)
        ]

    order = [start + i for runs in parts for start, number in runs for i in range(number)]
    for slot in range(min(AHEAD, len(order))):
        for copy in copies(order[slot], slot):
            copy.start()

    counting = pltpu.make_async_copy(counts_from, counts_ref, counted)
    counting.start()
    counting.wait()

    def later(slot):
        day, at = jnp.int32(0), 0
        for runs in parts:
            for start, number in runs:
                inside = (slot + AHEAD >= at) & (slot + AHEAD < at + number)
                day = jnp.where(inside, start + slot + AHEAD - at, day)
                at += number

        @pl.when(slot + AHEAD < len(order))
        def _():
            for copy in copies(day, slot + AHEAD):
                copy.start()

    slot = 0
    for runs, out_ref, sent_ref in zip(parts, outs, sents):
        days = length(runs)
        small = days * FULL
        out_ref[small:] = jnp.zeros((small_rows(days), LANES), jnp.float32)
        numbers = jnp.zeros((1, LANES), jnp.int32)
        at = 0
        for start, number in runs:

            def day(i, numbers, start=start, at=at, slot=slot, out_ref=out_ref, small=small):
                gram = jnp.zeros((width, width), jnp.float32)
                total = jnp.zeros((1, width), jnp.float32)
                later(slot + i)
                for copy in copies(start + i, slot + i):
                    copy.wait()
                for g in range(groups):
                    count = counts_ref[0, g, start + i]
                    numbers += jnp.where(lane == at + i, count, 0)
                    block = held[slot + i, g]
                    left = jnp.concatenate([block.T, jnp.ones((2 * SUBLANES, slots), block.dtype)], axis=0)
                    left = jnp.where(rank < count, left, jnp.zeros_like(left))
                    product = jnp.dot(left, block, preferred_element_type=jnp.float32)
                    gram += product[:width]
                    total += product[width : width + 1]
                base = pl.multiple_of((at + i) * FULL, FULL)
                low, diagonal_low = pack_quadrant(gram[:LANES, :LANES])
                high, diagonal_high = pack_quadrant(gram[LANES:, LANES:])
                out_ref[pl.ds(base, LANES)] = gram[:LANES, LANES:]
                out_ref[pl.ds(base + LANES, BLOCK)] = low
                out_ref[pl.ds(base + LANES + BLOCK, BLOCK)] = high
                row = small + SMALL * (at + i)
                out_ref[pl.ds(row, 1)] = diagonal_high + swap(diagonal_low)
                out_ref[pl.ds(row + 1, 1)] = total[:, :LANES]
                out_ref[pl.ds(row + 2, 1)] = total[:, LANES:]
                return numbers

            numbers = lax.fori_loop(0, number, day, numbers)
            at += number
            slot += number
        last = small + SMALL * days
        out_ref[last : last + 1] = numbers.astype(jnp.float32)
        pack_sent(days, low_half, out_ref, sent_ref)


def gram(samples, counts, year, parts, after):
    _, groups, slots, width = samples.shape
    days = sum(length(runs) for runs in parts)
    rows = [length(runs) * FULL + small_rows(length(runs)) for runs in parts]
    rows += [sent_rows(length(runs)) + small_rows(length(runs)) for runs in parts]
    outs, token = call(
        functools.partial(gram_kernel, parts),
        (counts, year, samples, after),
        (ANYWHERE, SCALARS, ANYWHERE, ANYWHERE),
        [(size, LANES) for size in rows],
        [
            pltpu.VMEM((days, groups, slots, width), samples.dtype),
            pltpu.SemaphoreType.DMA((days, groups)),
            pltpu.SMEM(counts.shape, counts.dtype),
            pltpu.SemaphoreType.DMA(()),
        ],
        2 * days * groups * slots * width * width,
        2 * days * groups * slots * width + 4 * sum(rows) * LANES,
        44,
    )
    return list(zip(outs[: len(parts)], outs[len(parts) :])), token


def inner_kernel(days, year_ref, mine_ref, came_ref, after_ref, send_ref, keep_ref, token_ref):
    low_half = year_ref[0] < 2
    token_ref[...] = jnp.zeros_like(token_ref)
    row, lane = iotas((BLOCK, LANES))
    at = sent_rows(days)

    def day(i, carry):
        src = pl.multiple_of(i * FULL, FULL)
        dst = pl.multiple_of(i * CROSS, CROSS)
        send_ref[pl.ds(dst, LANES)] = mine_ref[pl.ds(src, LANES)] + came_ref[pl.ds(dst, LANES)]
        other = pl.ds(dst + LANES, BLOCK)
        send_ref[other] = half_rows(mine_ref, i, ~low_half) + came_ref[other]
        return carry

    lax.fori_loop(0, days, day, 0)

    def pair(p, carry):
        src = pl.multiple_of(days * CROSS + p * PAIR, PAIR // 3)
        blocks = came_ref[pl.ds(src, BLOCK)]
        rest = came_ref[pl.ds(src + BLOCK, BLOCK // 2)]
        triangles = jnp.concatenate([rest, swap(rest)], axis=0)
        turned = jnp.concatenate([triangles, jnp.zeros_like(triangles)], axis=0).T[:BLOCK]
        side = jnp.where(low_half, row - lane, lane - row)
        for k, block in enumerate((swap(blocks), blocks)):
            i = 2 * p + k
            triangle = jnp.where(low_half, (triangles, turned)[k], (turned, triangles)[k])
            diagonal = jnp.where(low_half, 0.0, came_ref[pl.ds(at + SMALL * i, 1)])
            triangle = jnp.where(side > 0, triangle, jnp.where(side == 0, diagonal, 0.0))
            keep_ref[pl.ds(pl.multiple_of(i * BLOCK, BLOCK), BLOCK)] = half_rows(mine_ref, i, low_half) + jnp.where(
                lane < BLOCK, triangle, block
            )
        return carry

    lax.fori_loop(0, days // 2, pair, 0)
    if days % 2:
        last = at - BLOCK
        keep_ref[(days - 1) * BLOCK :] = half_rows(mine_ref, days - 1, low_half) + came_ref[last:at]
    row, lane = iotas((small_rows(days), LANES))
    diagonals = (lax.rem(row, SMALL) == 0) & (row < SMALL * days) & (lane < BLOCK)
    came = jnp.where(diagonals & ~low_half, 0.0, came_ref[at:])
    send_ref[days * CROSS :] = mine_ref[days * FULL :] + came


def inner(year, mine, came, days, after):
    rows = days * CROSS + small_rows(days)
    (send, keep), token = call(
        functools.partial(inner_kernel, days),
        (year, mine, came, after),
        (SCALARS, INSIDE, INSIDE, ANYWHERE),
        [(rows, LANES), (days * BLOCK, LANES)],
        [],
        days * FULL * LANES,
        3 * 4 * days * FULL * LANES,
    )
    return send, keep, token


def own_size(days):
    return days * OWN + small_rows(days)


def cross_kernel(sizes, year_ref, *refs):
    held, (_, send_ref, *owns, token_ref) = refs[: 3 * len(sizes)], refs[3 * len(sizes) :]
    low_half = year_ref[0] < 2
    token_ref[...] = jnp.zeros_like(token_ref)
    _, lane = iotas((BLOCK, LANES))
    base = 0
    for p, (days, own_ref) in enumerate(zip(sizes, owns)):
        mine_ref, keep_ref, came_ref = held[3 * p : 3 * p + 3]

        def day(i, carry, mine_ref=mine_ref, keep_ref=keep_ref, came_ref=came_ref, own_ref=own_ref, base=base):
            src = pl.multiple_of(i * CROSS, CROSS)
            own = pl.multiple_of(i * BLOCK, BLOCK)
            dst = pl.multiple_of(i * OWN, OWN)
            out = pl.multiple_of(base + i * OWN, SUBLANES)
            top = mine_ref[pl.ds(src, BLOCK)] + came_ref[pl.ds(src, BLOCK)]
            bottom = mine_ref[pl.ds(src + BLOCK, BLOCK)] + came_ref[pl.ds(src + BLOCK, BLOCK)]
            packed = keep_ref[pl.ds(own, BLOCK)] + came_ref[pl.ds(src + LANES, BLOCK)]
            first = jnp.where(lane < BLOCK, top, swap(bottom))
            second = jnp.where(lane < BLOCK, swap(top), bottom)
            send_ref[pl.ds(out, BLOCK)] = packed
            own_ref[pl.ds(dst, BLOCK)] = packed
            send_ref[pl.ds(out + BLOCK, BLOCK)] = jnp.where(low_half, top, second)
            own_ref[pl.ds(dst + BLOCK, BLOCK)] = jnp.where(low_half, bottom, first)
            return carry

        lax.fori_loop(0, days, day, 0)
        small = mine_ref[days * CROSS :] + came_ref[days * CROSS :]
        send_ref[base + days * OWN : base + own_size(days)] = small
        own_ref[days * OWN :] = small
        base += own_size(days)


def cross(year, held, sizes, after):
    rows = [own_size(days) for days in sizes]
    (send, *owns), token = call(
        functools.partial(cross_kernel, sizes),
        (year, *(array for arrays in held for array in arrays), after),
        [SCALARS] + [INSIDE] * (3 * len(sizes)) + [ANYWHERE],
        [(sum(rows), LANES)] + [(size, LANES) for size in rows],
        [],
        sum(sizes) * CROSS * LANES,
        3 * 4 * sum(sizes) * CROSS * LANES,
    )
    return send, owns, token


def is_outer(year):
    return (year == 0) | (year == 3)


def day_rows(year, number, i, mine_ref, own_ref, came_ref):
    outer, low_half = is_outer(year), year < 2
    row, lane = iotas((BLOCK, LANES))
    alone = jnp.where(own_side(row, lane, low_half), half_rows(mine_ref, i, low_half), 0.0)
    start = i * OWN
    top = jnp.where(outer, came_ref[start : start + BLOCK] + alone, own_ref[start : start + BLOCK])
    middle = start + BLOCK
    bottom = jnp.where(outer, came_ref[middle : middle + BLOCK], own_ref[middle : middle + BLOCK])
    at = number * OWN + SMALL * i
    small = jnp.where(outer, came_ref[at : at + SMALL], own_ref[at : at + SMALL])
    kept = mine_ref[number * FULL + SMALL * i : number * FULL + SMALL * i + 1]
    diagonal = small[:1] + jnp.where(outer & ~low_half & (lane[:1] < BLOCK), kept, 0.0)
    return jnp.concatenate([top, bottom], axis=0), diagonal, small[1:2], small[2:3]


def day_counts(year, number, own_ref, came_ref):
    at = number * OWN + SMALL * number
    return jnp.where(is_outer(year), came_ref[at : at + 1], own_ref[at : at + 1])


def views(refs, bases, sizes):
    held = []
    for p, (base, size) in enumerate(zip(bases, sizes)):
        mine_ref, own_ref, came_ref = refs[3 * p : 3 * p + 3]
        held.append((mine_ref, own_ref, came_ref.at[pl.ds(base, own_size(size))]))
    return held


def pick_kernel(bases, sizes, moves, year_ref, *refs):
    held = views(refs, bases, sizes)
    (_, *outs, token_ref) = refs[3 * len(sizes) :]
    year = year_ref[0]
    token_ref[...] = jnp.zeros_like(token_ref)
    lane = lax.broadcasted_iota(jnp.int32, (1, LANES), 1)
    counts = [day_counts(year, size, *arrays[1:]) for size, arrays in zip(sizes, held)]
    for stretch, out_ref in zip(moves, outs):
        small = len(stretch) * OWN
        numbers = jnp.zeros((1, LANES), jnp.float32)
        for k, (p, i) in enumerate(stretch):
            rows, *lines = day_rows(year, sizes[p], i, *held[p])
            out_ref[k * OWN : (k + 1) * OWN] = rows
            for l, line in enumerate(lines):
                at = small + SMALL * k + l
                out_ref[at : at + 1] = line
            number = jnp.sum(jnp.where(lane == i, counts[p], 0.0), axis=1, keepdims=True)
            numbers += jnp.where(lane == k, number, 0.0)
        last = small + SMALL * len(stretch)
        out_ref[last : last + 1] = numbers


def pick(year, held, bases, sizes, moves, after):
    return call(
        functools.partial(pick_kernel, bases, sizes, moves),
        (year, *(array for arrays in held for array in arrays), after),
        [SCALARS] + [INSIDE] * (3 * len(sizes)) + [ANYWHERE],
        [(own_size(len(stretch)), LANES) for stretch in moves],
        [],
        0,
        2 * 4 * sum(sizes) * OWN * LANES,
    )


def unpack(year, rows, diagonal):
    odd = lax.rem(year, 2) == 1
    low_half = year < 2
    row, lane = iotas((BLOCK, LANES))
    turned = rows.T
    top, bottom = rows[:BLOCK], rows[BLOCK:]
    top_turned, bottom_turned = turned[:BLOCK], turned[BLOCK:]
    upper = jnp.where(lane < BLOCK, jnp.where(row <= lane, top, top_turned), top)
    lower = swap(jnp.where(row > lane, top, top_turned))
    diagonal = jnp.where(low_half, diagonal, swap(diagonal))
    lower = jnp.where(row == lane - BLOCK, diagonal, lower)
    lower = jnp.where(lane < BLOCK, bottom_turned, lower)
    packed = jnp.where(odd, lower, upper)
    across = jnp.where(lane < BLOCK, swap(top_turned), bottom_turned)
    return jnp.where(low_half, packed, across), jnp.where(low_half, bottom, packed)


def windows_kernel(places, days, year_ref, *refs):
    parts = refs[: len(places)]
    win_ref, small_ref, token_ref, packed_ref = refs[len(places) + 1 :]
    token_ref[...] = jnp.zeros_like(token_ref)
    year = year_ref[0]
    extended = days + 2 * HALF
    where = {}
    for (place, number), ref in zip(places, parts):
        for i in range(number):
            where[place + i] = (ref, i, number * OWN)

    def sums(load, store):
        def add(a, b):
            return b if a is None else a if b is None else a + b

        def level(table, hop):
            return [add(table[k], table[k + hop]) for k in range(len(table) - hop)]

        ones = [load(*where[k]) if k in where else None for k in range(extended)]
        twos = level(ones, 1)
        fours = level(twos, 2)
        eights = level(fours, 4)
        for d in range(days):
            store(d, add(add(eights[d], fours[d + 8]), add(twos[d + 12], ones[d + 14])))

    def strip(s, carry):
        at = pl.multiple_of(s * SUBLANES, SUBLANES)

        def store(d, value):
            packed_ref[d, pl.ds(at, SUBLANES)] = value

        sums(lambda ref, i, small: ref[pl.ds(i * OWN + at, SUBLANES)], store)
        return carry

    lax.fori_loop(0, OWN // SUBLANES, strip, 0)

    for row in range(SMALL):

        def store_row(d, value):
            small_ref[row, d : d + 1] = value

        sums(lambda ref, i, small: ref[small + SMALL * i + row : small + SMALL * i + row + 1], store_row)

    lane = lax.broadcasted_iota(jnp.int32, (1, LANES), 1)

    def load_count(ref, i, small):
        last = small + SMALL * (small // OWN)
        count = jnp.sum(jnp.where(lane == i, ref[last : last + 1], 0.0), axis=1, keepdims=True)
        return jnp.broadcast_to(count, (1, LANES))

    def store_count(d, value):
        small_ref[SMALL, d : d + 1] = value

    sums(load_count, store_count)

    def day(d, carry):
        left, right = unpack(year, packed_ref[d], small_ref[0, pl.ds(d, 1)])
        win_ref[d, :, :LANES] = left
        win_ref[d, :, LANES:] = right
        return carry

    lax.fori_loop(0, days, day, 0, unroll=True)


def windows(year, parts, places, days, after):
    (win, small), token = call(
        functools.partial(windows_kernel, places, days),
        (year, *parts, after),
        [SCALARS] + [INSIDE] * len(parts) + [ANYWHERE],
        [(days, BLOCK, 2 * LANES), (SMALL + 1, days, LANES)],
        [pltpu.VMEM((days, OWN, LANES), jnp.float32)],
        6 * days * BLOCK * 2 * LANES,
        8 * days * BLOCK * 2 * LANES,
    )
    return win, small, token


def finish_kernel(bases, places, pieces, year_ref, win_ref, small_ref, *refs):
    held = views(refs, bases, [number for _, number in places])
    after_ref, cov_ref, mean_ref, token_ref, formed, sent = refs[3 * len(places) :]
    token_ref[...] = jnp.zeros_like(token_ref)
    year = year_ref[0]
    days = win_ref.shape[0]
    lane = lax.broadcasted_iota(jnp.int32, (1, LANES), 1)
    day_of = lax.broadcasted_iota(jnp.int32, (days, LANES), 0)
    low, high, count = small_ref[1], small_ref[2], small_ref[SMALL]
    extras = []
    for p, (place, number) in enumerate(places):
        arrays = held[p]
        numbers = day_counts(year, number, *arrays[1:])
        for i in range(number):
            rows, diagonal, more_low, more_high = day_rows(year, number, i, *arrays)
            inside = jnp.abs(day_of - (place + i)) <= HALF
            low += jnp.where(inside, more_low, 0.0)
            high += jnp.where(inside, more_high, 0.0)
            extra = jnp.sum(jnp.where(lane == i, numbers, 0.0), axis=1, keepdims=True)
            count += jnp.where(inside, extra, 0.0)
            extras.append((place + i, unpack(year, rows, diagonal)))
    low = low / count
    high = high / count
    own = jnp.where(year < 2, low, high)
    own = jnp.where(lax.rem(year, 2) == 1, swap(own), own)
    mean_ref[:, 0] = own[:, :BLOCK]
    turned = jnp.concatenate([own, jnp.zeros((LANES - days, LANES), jnp.float32)], axis=0).T
    scale = 1.0 / (count - 1.0)
    low = low * (count * scale)
    high = high * (count * scale)
    copies = []
    for first, size in pieces:
        for d in range(first, first + size):
            left, right = win_ref[d, :, :LANES], win_ref[d, :, LANES:]
            for at, (more_left, more_right) in extras:
                if abs(d - at) <= HALF:
                    left, right = left + more_left, right + more_right
            column = turned[:BLOCK, d : d + 1]
            factor = scale[d : d + 1]
            formed[d, :, :LANES] = left * factor - column * low[d : d + 1]
            formed[d, :, LANES:] = right * factor - column * high[d : d + 1]
        piece = pl.ds(first, size)
        copy = pltpu.make_async_copy(formed.at[piece], cov_ref.at[0, piece], sent.at[len(copies)])
        copy.start()
        copies.append(copy)
    for copy in copies:
        copy.wait()


def finish(year, win, small, held, bases, places, after):
    days, _, width = win.shape
    size = -(-days // 6)
    pieces = tuple((first, min(size, days - first)) for first in range(0, days, size))
    flat = [array for arrays in held for array in arrays]
    (covariance, mean), _ = call(
        functools.partial(finish_kernel, bases, places, pieces),
        (year, win, small, *flat, after),
        [SCALARS] + [INSIDE] * (2 + len(flat)) + [ANYWHERE],
        [(1, days, BLOCK, width), (days, 1, BLOCK)],
        [pltpu.VMEM((days, BLOCK, width), jnp.float32), pltpu.SemaphoreType.DMA((len(pieces),))],
        6 * days * BLOCK * width,
        8 * days * BLOCK * width,
        outs=[ANYWHERE, INSIDE],
    )
    return covariance, mean


def plan(days):
    parts = [((0, 4),), ((days - 5, 5),), ((4, HALF - 4), (days - HALF, HALF - 5))]
    at, left = HALF, days - 2 * HALF
    for size in (left - 5, 3, 2):
        parts.append(((at, size),))
        at += size
    return parts


ORDER = (
    ("gram", 0),
    ("gram", 1),
    ("gram", 2),
    ("inner", 0),
    ("gram", 3, 4, 5),
    ("inner", 1),
    ("cross", 0),
    ("inner", 2),
    ("pick", 0),
    ("cross", 1),
    ("inner", 3),
    ("pick", 1),
    ("cross", 2),
    ("inner", 4),
    ("cross", 3),
    ("pick", 2),
    ("inner", 5),
    ("cross", 4),
    ("cross", 5),
    ("pick", 3),
    ("windows",),
    ("finish", 4, 5),
)


def shards(samples, counts):
    days = samples.shape[0]
    day_size = lax.axis_size("day")
    position = lax.axis_index("year")
    year = position.astype(jnp.int32)[None]
    inward = [(0, 1), (3, 2)]
    between = [(1, 2), (2, 1)]
    outward = [(1, 0), (2, 3)]
    right = [(i, (i + 1) % day_size) for i in range(day_size)]
    left = [((i + 1) % day_size, i) for i in range(day_size)]
    counts = jnp.transpose(counts, (0, 2, 1))
    parts = plan(days)
    token = jnp.zeros(TOKEN, jnp.float32)
    mine, sums, rows = {}, {}, {}
    totals, places, bases = [], [], {}

    def gram_step(*ks):
        nonlocal token
        outs, token = gram(samples, counts, year, tuple(parts[k] for k in ks), token)
        for k, (out, sent) in zip(ks, outs):
            mine[k] = (out, lax.ppermute(sent, "year", inward))

    def inner_step(k):
        nonlocal token
        send, keep, token = inner(year, *mine[k], length(parts[k]), token)
        sums[k] = (send, keep, lax.ppermute(send, "year", between))

    def cross_step(*ks):
        nonlocal token
        sizes = [length(parts[k]) for k in ks]
        send, owns, token = cross(year, [sums[k] for k in ks], sizes, token)
        came = lax.ppermute(send, "year", outward)
        base = 0
        for k, own, size in zip(ks, owns, sizes):
            rows[k] = (mine[k][0], own, came)
            bases[k] = base
            base += own_size(size)

    def pick_step(*ks):
        nonlocal token
        found = {}
        for p, k in enumerate(ks):
            at = 0
            for start, size in parts[k]:
                found.update({start + i: (p, at + i) for i in range(size)})
                at += size
        low = [day for day in sorted(found) if day < HALF]
        high = [day for day in sorted(found) if day >= days - HALF]
        inside = [day for day in sorted(found) if HALF <= day < days - HALF]
        stretches = [stretch for stretch in (low, high, inside) if stretch]
        moves = [[found[day] for day in stretch] for stretch in stretches]
        sizes = [length(parts[k]) for k in ks]
        outs, token = pick(year, [rows[k] for k in ks], [bases[k] for k in ks], sizes, moves, token)
        for stretch, out in zip(stretches, outs):
            start, size = stretch[0], len(stretch)
            totals.append(out)
            places.append((start + HALF, size))
            if start < HALF:
                totals.append(lax.ppermute(out, "day", left))
                places.append((start + HALF + days, size))
            elif start >= days - HALF:
                totals.append(lax.ppermute(out, "day", right))
                places.append((start + HALF - days, size))

    def windows_step():
        nonlocal token
        win, small, token = windows(year, totals, tuple(places), days, token)
        return win, small

    def finish_step(*ks):
        last = tuple(parts[k][0] for k in ks)
        return finish(year, *held, [rows[k] for k in ks], [bases[k] for k in ks], last, token)

    steps = {
        "gram": gram_step,
        "inner": inner_step,
        "cross": cross_step,
        "pick": pick_step,
        "windows": windows_step,
        "finish": finish_step,
    }
    held = None
    for name, *ks in ORDER:
        result = steps[name](*ks)
        held = result if result else held
    covariance, mean = held
    return covariance, jnp.transpose(mean, (1, 0, 2))


def solution(mesh):
    placed = (P("day", "year", "region", None), P("region", "day", "year"))
    return jax.shard_map(
        shards,
        mesh=mesh,
        in_specs=placed,
        out_specs=(P("region", "day", "year", None), P("region", "day", "year")),
        check_vma=False,
    )
```
